128 devices in a mesh: seq: 32 (over z_hi, y, x), kv: 4 (over z_lo, core).
Axes of the slice: x: 4, y: 4, z: 4 (z_hi: 2, z_lo: 2; z = z_hi * 2 + z_lo), core: 2. Of those that a mesh axis runs over, the one named last changes fastest.
Arguments:
- queries: bfloat16 [8192, 3584], P('seq', 'kv'), may hold values from -36 to 36
- keys: bfloat16 [8192, 512], P('seq', 'kv'), may hold values from -6 to 6
- values: bfloat16 [8192, 512], P('seq', 'kv'), may hold values from -6 to 6
- doc_lengths: int32 [16], replicated, may hold values from 1 to 68, 128 in all
- out_weight: bfloat16 [3584, 3584], P(None, 'kv'), may hold values from -0.796875 to 0.796875
Outputs:
- mixed: bfloat16 [8192, 3584], P('seq', 'kv')
The draws below stay inside these ranges and needn't reach their ends.
Inputs may be any that keep to these rules, and one draw needn't show every extreme that they name: `doc_lengths`: the lengths sum to 128 and the largest is exactly 68.
All inputs are finite; a program needn't handle non-finite values.
Results may differ from the reference program's by a relative error of at most 0.009.
Values may be sent and summed in bfloat16 or wider, within the bound.
No kernel may reach another device: no remote copies, remote signals or barrier semaphores. Data moves between devices by JAX's collectives and lax.ppermute only.
A program may use at most 64 MiB of HBM per device.

```python
import math
import jax
import jax.numpy as jnp
import numpy as np
from jax import lax

D = 3584
QH = 28
KVH = 4
HD = 128
TOK_DEV = 256
GRAIN = 64
SEQ = 8192
DOC_MOST = 4352
DOCS = 16


def draw_keys(key, part):
    key = jax.random.fold_in(key, 11)
    result = jax.random.normal(key, (SEQ, KVH * HD), jnp.float32)
    result = jnp.clip(result, -6.0, 6.0)
    return result.astype(jnp.bfloat16)


def draw_queries(key, part):
    key = jax.random.fold_in(key, 12)
    result = 1.5 * jax.random.normal(key, (SEQ, QH * HD), jnp.float32)
    result = jnp.clip(result, -9.0, 9.0)
    return result.astype(jnp.bfloat16)


def steps_of(rng, shape, split, low, largest):
    loudness = 1.0
    for axis_at, parts in split:
        steps = jax.random.uniform(jax.random.fold_in(jax.random.fold_in(rng, 6), axis_at), (parts,), jnp.float32, low / len(split), largest / len(split))
        loudness = loudness * jnp.repeat(jnp.exp(steps), shape[axis_at] // parts).reshape((-1,) + (1,) * (len(shape) - 1 - axis_at))
    return loudness


def length_profile(count, total, reach, skew):
    portions = [(1 << 20) // math.isqrt(grade ** skew) + 1 for grade in range(2, count + 1)]
    spare, given = total - reach - (count - 1), [1] * (count - 1)
    while spare > 0:
        movable = [i for i in range(count - 1) if given[i] < reach]
        mass, remaining = sum([portions[i] for i in movable]), spare
        for i in movable:
            more = min(reach - given[i], max(1, remaining * portions[i] // mass), spare)
            given[i] = given[i] + more
            spare = spare - more
    return np.array([reach] + given)


def ragged_sizes(own_key, count, total, bound, skew):
    if count == 2:
        one = jax.random.randint(own_key, (), max(1, total - bound), min(bound, total - 1) + 1)
        return jnp.stack([one, total - one])
    sizes = jnp.asarray(length_profile(count, total, bound, skew), jnp.int32)
    couples = (count - 1) // 2
    source_of, taker = sizes[1:1 + 2 * couples:2], sizes[2:2 + 2 * couples:2]
    margin = jnp.minimum(source_of - 1, bound - taker)
    moved = jax.random.randint(jax.random.fold_in(own_key, 1), (couples,), 0, 1 << 20) % (margin + 1)
    sizes = sizes.at[1:1 + 2 * couples:2].set(source_of - moved).at[2:2 + 2 * couples:2].set(taker + moved)
    return sizes[jax.random.permutation(jax.random.fold_in(own_key, 2), count)]


def scatter_about(stream_key, extent, scale, limit, pieces=(), kind=jnp.bfloat16):
    values = jax.random.normal(stream_key, extent, jnp.float32) * scale
    if len(pieces) > 0:
        values = steps_of(stream_key, extent, pieces, -0.22, 0.18) * values
    return jnp.clip(values, min=-limit, max=limit).astype(kind)


def setup_inputs(seed: int = 0) -> dict:
    key_of = jax.random.split(jax.random.key(seed), 6)
    queries = draw_queries(jax.random.fold_in(key_of[5], 71), 0)
    keys = draw_keys(jax.random.fold_in(key_of[5], 71), 0)
    values = scatter_about(key_of[2], (SEQ, KVH * HD), 1.0, 6.0, ((0, 32), (1, 4)))
    doc_lengths = ragged_sizes(key_of[3], DOCS, SEQ // GRAIN, DOC_MOST // GRAIN, 1).astype(jnp.int32)
    out_weight = scatter_about(key_of[4], (QH * HD, D), 0.134, 0.796875, ((1, 4),))
    return dict(queries=queries, keys=keys, values=values, doc_lengths=doc_lengths, out_weight=out_weight)


def document_of(positions, doc_ends):
    return jnp.sum((doc_ends[None, :] <= positions[:, None]).astype(jnp.int32), axis=1).astype(jnp.int32)


def reference(queries, keys, values, doc_lengths, out_weight):
    doc_ends = (jnp.cumsum(doc_lengths) * GRAIN).astype(jnp.int32)
    doc_all = document_of(jnp.arange(SEQ, dtype=jnp.int32), doc_ends)
    window = min(SEQ, TOK_DEV + 2 * DOC_MOST)
    per_group = QH // KVH
    score_scale = 1.0 / (HD ** 0.5)

    def one_block(block_index):
        q_start = (block_index * TOK_DEV).astype(jnp.int32)
        k_start = jnp.clip(q_start - DOC_MOST, 0, SEQ - window).astype(jnp.int32)
        q_doc = lax.dynamic_slice_in_dim(doc_all, q_start, TOK_DEV, 0)
        k_doc = lax.dynamic_slice_in_dim(doc_all, k_start, window, 0)
        allowed = (q_doc[:, None] == k_doc[None, :])[None]
        q_rows = lax.dynamic_slice_in_dim(queries, q_start, TOK_DEV, 0)
        k_rows = lax.dynamic_slice_in_dim(keys, k_start, window, 0)
        v_rows = lax.dynamic_slice_in_dim(values, k_start, window, 0)
        outputs = []
        for head_group in range(KVH):
            q_part = q_rows[:, head_group * per_group * HD:(head_group + 1) * per_group * HD]
            q_part = q_part.reshape(TOK_DEV, per_group, HD).astype(jnp.float32)
            k_part = k_rows[:, head_group * HD:(head_group + 1) * HD].astype(jnp.float32)
            v_part = v_rows[:, head_group * HD:(head_group + 1) * HD].astype(jnp.float32)
            scores = jnp.einsum("qhd,td->hqt", q_part, k_part) * score_scale
            masked = jnp.where(allowed, scores, -jnp.inf)
            peak = jnp.max(masked, axis=-1, keepdims=True)
            expo = jnp.where(allowed, jnp.exp(masked - peak), 0.0)
            total = jnp.sum(expo, axis=-1)
            weights = expo.astype(jnp.bfloat16).astype(jnp.float32)
            summed = jnp.einsum("hqt,td->hqd", weights, v_part)
            result = summed / total[..., None]
            outputs.append(jnp.transpose(result, (1, 0, 2)).reshape(TOK_DEV, per_group * HD))
        return jnp.concatenate(outputs, axis=1).astype(jnp.bfloat16)

    blocks = lax.map(one_block, jnp.arange(SEQ // TOK_DEV, dtype=jnp.int32))
    attended = blocks.reshape(SEQ, QH * HD)
    return jnp.dot(attended, out_weight, preferred_element_type=jnp.float32).astype(jnp.bfloat16)
```

```python
import jax
import jax.numpy as jnp
import numpy as np
from jax import lax
from jax.experimental import pallas as pl
from jax.experimental.pallas import tpu as pltpu
from jax.sharding import Mesh, PartitionSpec as P

HD = 128
GRAIN = 64
TOK = 256
HEADS = 7
SEQ = 8192
DOCS = 16
LONG = 4352
LONG_GRAINS = LONG // GRAIN
GRAINS = TOK // GRAIN
ROWS = HEADS * GRAIN
HALF = LONG // 2
SMALL = 256
SCALE = 1.4426950408889634 / HD**0.5
LOWEST = -1e30
PLANE = ("y", "x", "c")
OFFSETS = (0, -1, 1, 2)


def turn(by_first, by_second):
    pairs = []
    for y in range(4):
        for x in range(4):
            pairs.append((y, x, 0, (y + by_first) % 4, (x + by_second) % 4))
            pairs.append((y, x, 1, (y + by_second) % 4, (x + by_first) % 4))
    return [((y * 4 + x) * 2 + c, (to_y * 4 + to_x) * 2 + c) for y, x, c, to_y, to_x in pairs]


def swap(block, axis):
    return lax.ppermute(block, axis, [(0, 1), (1, 0)])


def softmax_step(state, query, keys, values, allowed):
    peak, summed = state
    scores = lax.dot_general(
        query, keys, (((1,), (1,)), ((), ())), preferred_element_type=jnp.float32
    )
    scores = scores * SCALE
    if allowed is not None:
        scores = jnp.where(allowed, scores, LOWEST)
    peak_new = jnp.maximum(peak, jnp.max(scores, axis=1, keepdims=True))
    weights = jnp.exp2(scores - peak_new).astype(jnp.bfloat16)
    product = jnp.dot(weights, values, preferred_element_type=jnp.float32)
    return peak_new, summed * jnp.exp2(peak - peak_new) + product


def attend_kernel(lengths, place, queries, b0, b1, b2, b3, out, keys, values, sems, rows, result):
    zh, y, x, c = place[0], place[1], place[2], place[3]
    copies = []
    for outer, (ref, far) in enumerate(zip((b0, b1, b2, b3), OFFSETS)):
        for inner, near in enumerate(OFFSETS):
            up = jnp.where(c == 0, far, near)
            across = jnp.where(c == 0, near, far)
            for other in range(2):
                plane = zh ^ other
                at = plane * 16 + ((y + up + 4) % 4) * 4 + (x + across + 4) % 4
                at = pl.multiple_of(at * TOK, TOK)
                src = pl.ds((inner * 2 + other) * TOK, TOK)
                copies.append(pltpu.make_async_copy(
                    ref.at[src, pl.ds(0, HD)], keys.at[pl.ds(at, TOK), :], sems.at[0, outer * 8 + inner * 2 + other]))
                copies.append(pltpu.make_async_copy(
                    ref.at[src, pl.ds(HD, HD)], values.at[pl.ds(at, TOK), pl.ds(0, HD)], sems.at[1, outer * 8 + inner * 2 + other]))
    for copy in copies:
        copy.start()
    values[:, HD:] = jnp.ones((SEQ + SMALL, HD), jnp.bfloat16)
    values[SEQ:, :HD] = jnp.zeros((SMALL, HD), jnp.bfloat16)
    for grain in range(GRAINS):
        for head in range(HEADS):
            rows[pl.ds(grain * ROWS + head * GRAIN, GRAIN), :] = queries[
                pl.ds(grain * GRAIN, GRAIN), pl.ds(head * HD, HD)]
    for copy in copies:
        copy.wait()

    first_grain = ((zh * 4 + y) * 4 + x) * GRAINS

    def one_grain(grain, carry):
        at = first_grain + grain
        begin, end, total = jnp.int32(0), jnp.int32(0), jnp.int32(0)
        for doc in range(DOCS):
            after = total + lengths[doc]
            here = (total <= at) & (at < after)
            begin = jnp.where(here, total, begin)
            end = jnp.where(here, after, end)
            total = after
        span = pl.ds(pl.multiple_of(grain * ROWS, ROWS), ROWS)
        is_long = end - begin == LONG_GRAINS
        initial = (jnp.full((ROWS, 1), LOWEST, jnp.float32), jnp.zeros((ROWS, 2 * HD), jnp.float32))

        def finish(summed):
            result[...] = (summed[:, :HD] / summed[:, HD:]).astype(jnp.bfloat16)
            for head in range(HEADS):
                out[pl.ds(pl.multiple_of(grain * GRAIN, GRAIN), GRAIN), pl.ds(head * HD, HD)] = result[
                    pl.ds(head * GRAIN, GRAIN), :]

        @pl.when(is_long)
        def _():
            query, state = rows[span, :], initial
            for half in range(2):
                part = pl.ds(pl.multiple_of(begin * GRAIN + half * HALF, GRAIN), HALF)
                state = softmax_step(state, query, keys[part, :], values[part, :], None)
            finish(state[1])

        @pl.when(jnp.logical_not(is_long))
        def _():
            query = rows[span, :]
            column = lax.broadcasted_iota(jnp.int32, (1, SMALL), 1)

            def step(index, state):
                start = begin * GRAIN + index * SMALL
                part = pl.ds(pl.multiple_of(start, GRAIN), SMALL)
                return softmax_step(
                    state, query, keys[part, :], values[part, :], column < end * GRAIN - start)

            steps = ((end - begin) * GRAIN + SMALL - 1) // SMALL
            finish(lax.fori_loop(0, steps, step, initial)[1])

        return carry

    lax.fori_loop(0, GRAINS, one_grain, 0)


def attend(lengths, place, queries, blocks):
    smem = pl.BlockSpec(memory_space=pltpu.SMEM)
    vmem = pl.BlockSpec(memory_space=pltpu.VMEM)
    hbm = pl.BlockSpec(memory_space=pl.ANY)
    return pl.pallas_call(
        attend_kernel,
        out_shape=jax.ShapeDtypeStruct((TOK, HEADS * HD), jnp.bfloat16),
        in_specs=[smem, smem, vmem] + [hbm] * 4,
        out_specs=vmem,
        scratch_shapes=[
            pltpu.VMEM((SEQ + SMALL, HD), jnp.bfloat16),
            pltpu.VMEM((SEQ + SMALL, 2 * HD), jnp.bfloat16),
            pltpu.SemaphoreType.DMA((2, 32)),
            pltpu.VMEM((GRAINS * ROWS, HD), jnp.bfloat16),
            pltpu.VMEM((ROWS, HD), jnp.bfloat16),
        ],
        compiler_params=pltpu.CompilerParams(vmem_limit_bytes=48 * 2**20),
    )(lengths, place, queries, *blocks)


def per_device(queries, keys, values, doc_lengths, out_weight):
    zh, y, x, zl, c = (lax.axis_index(a) for a in ("zh", "y", "x", "zl", "c"))
    own = jnp.concatenate([keys, values], axis=1)
    pair = jnp.concatenate([own, swap(own, "zh")], axis=0)
    near = jnp.concatenate(
        [pair] + [lax.ppermute(pair, PLANE, turn(0, -k)) for k in OFFSETS[1:]], axis=0
    )
    blocks = [near] + [lax.ppermute(near, PLANE, turn(-k, 0)) for k in OFFSETS[1:]]
    place = jnp.stack([zh, y, x, c]).astype(jnp.int32)
    attended = attend(doc_lengths, place, queries, blocks)
    across = swap(attended, "zl")
    parts = [attended, swap(attended, "c"), across, swap(across, "c")]
    group = zl * 2 + c
    weight = out_weight.reshape(4, HEADS * HD, out_weight.shape[1])
    mixed = 0.0
    for index, part in enumerate(parts):
        mixed = mixed + jnp.dot(
            part,
            lax.dynamic_index_in_dim(weight, group ^ index, 0, keepdims=False),
            preferred_element_type=jnp.float32,
        )
    return mixed.astype(jnp.bfloat16)


def solution(mesh):
    fine = Mesh(np.asarray(mesh.devices).reshape(2, 4, 4, 2, 2), ("zh", "y", "x", "zl", "c"))
    seq, kv = ("zh", "y", "x"), ("zl", "c")
    return jax.shard_map(
        per_device,
        mesh=fine,
        in_specs=(P(seq, kv), P(seq, kv), P(seq, kv), P(), P(None, kv)),
        out_specs=P(seq, kv),
        check_vma=False,
    )
```

```python
import functools

import jax
import jax.numpy as jnp
import numpy as np
from jax import lax
from jax.experimental import pallas as pl
from jax.experimental.pallas import tpu as pltpu
from jax.sharding import Mesh, PartitionSpec as P

HD = 128
GRAIN = 64
TOK = 256
HEADS = 7
GRAINS = TOK // GRAIN
DOCS = 16
LONG_GRAINS = 68
PLANE_GRAINS = 64
PLANE_TOK = PLANE_GRAINS * GRAIN
EXTRA = LONG_GRAINS - PLANE_GRAINS
PIECE = 4 * TOK
MESSAGE = PIECE + EXTRA * GRAIN
SMALL = 256
NEAR_BLOCKS = 3
FAR_BLOCKS = 9
FIRST_HEADS = 2
SCALE = 1.4426950408889634 / HD**0.5
LOWEST = -1e30
OFFSETS = (0, -1, 1, 2)

SMEM = pl.BlockSpec(memory_space=pltpu.SMEM)
VMEM = pl.BlockSpec(memory_space=pltpu.VMEM)
HBM = pl.BlockSpec(memory_space=pl.ANY)


def turn(by_first, by_second):
    pairs = []
    for y in range(4):
        for x in range(4):
            pairs.append((y, x, 0, (y + by_first) % 4, (x + by_second) % 4))
            pairs.append((y, x, 1, (y + by_second) % 4, (x + by_first) % 4))
    return [((y * 4 + x) * 2 + c, (to_y * 4 + to_x) * 2 + c) for y, x, c, to_y, to_x in pairs]


def move(block, by_first, by_second):
    return lax.ppermute(block, ("y", "x", "c"), turn(by_first, by_second))


def ring(block, step):
    pairs = []
    for at in range(16):
        pairs.append((at, (at + step) % 16))
        pairs.append((16 + at, 16 + (at - step) % 16))
    return lax.ppermute(block, ("zh", "y", "x"), pairs)


def swap(block, axis):
    return lax.ppermute(block, axis, [(0, 1), (1, 0)])


class Place:
    def __init__(self, place, lengths):
        self.zh, y, x, self.core = place[0], place[1], place[2], place[3]
        self.inner = jnp.where(self.core == 0, x, y)
        self.outer = jnp.where(self.core == 0, y, x)
        self.position = y * 4 + x
        total, start = jnp.int32(0), jnp.int32(0)
        for doc in range(DOCS):
            start = jnp.where(lengths[doc] == LONG_GRAINS, total, start)
            total = total + lengths[doc]
        self.start, self.stop = start, start + EXTRA

    def at(self, outer_by, inner_by):
        outer, inner = (self.outer + outer_by + 4) % 4, (self.inner + inner_by + 4) % 4
        return jnp.where(self.core == 0, outer * 4 + inner, inner * 4 + outer)

    def has_long(self, position):
        return jnp.where(self.zh == 0, position * 4 + 3 >= self.start, position * 4 < self.stop)

    def has_small(self, position):
        return jnp.where(self.zh == 0, position * 4 < self.start, position * 4 + 3 >= self.stop)

    def half(self, plane):
        return pl.multiple_of((plane ^ self.zh) * TOK, TOK)


def rows_of(start, count):
    return pl.ds(pl.multiple_of(start, GRAIN), count)


def start_long(here, position, pair, copy):
    cut = jnp.clip(here.start - position * 4, 0, 4)
    whole = (cut == 0) | (cut == 4)

    @pl.when(whole)
    def _():
        copy(rows_of(here.half((cut == 4).astype(jnp.int32)), TOK), 0)

    @pl.when(jnp.logical_not(whole))
    def _():
        for grain in range(GRAINS):
            plane = (grain < cut).astype(jnp.int32)
            copy(rows_of(here.half(plane) + grain * GRAIN, GRAIN), grain * GRAIN)


def pack_kernel(lengths, place, p0, p1, p2, p3, m1, m2, m3, sems):
    here = Place(place, lengths)
    pairs = (p0, p1, p2, p3)

    def extras(action):
        for extra in range(EXTRA):
            grain = here.start + extra
            for inner, pair in enumerate(pairs):
                @pl.when(grain // 4 == here.at(0, OFFSETS[inner]))
                def _():
                    action(extra, pair, rows_of(here.half(1) + grain % 4 * GRAIN, GRAIN))

    for index, out in enumerate((m1, m2, m3)):
        to_long = here.has_long(here.at(-OFFSETS[index + 1], 0))

        def copy(pair, source, target, slot):
            pltpu.make_async_copy(pair.at[source, :], out.at[target, :], sems.at[index, slot]).start()

        @pl.when(to_long)
        def _():
            for inner, pair in enumerate(pairs):
                start_long(
                    here, here.at(0, OFFSETS[inner]), pair,
                    lambda source, target: copy(pair, source, pl.ds(inner * TOK + target, source.size), inner),
                )
            extras(lambda extra, pair, source: copy(
                pair, source, pl.ds(PIECE + extra * GRAIN, GRAIN), 4 + extra))

        @pl.when(jnp.logical_not(to_long))
        def _():
            for inner, pair in enumerate(pairs):
                copy(pair, pl.ds(0, TOK), pl.ds(inner * TOK, TOK), inner)

    for index, out in enumerate((m1, m2, m3)):
        for inner, pair in enumerate(pairs):
            rows = pl.ds(inner * TOK, TOK)
            pltpu.make_async_copy(pair.at[pl.ds(0, TOK), :], out.at[rows, :], sems.at[index, inner]).wait()

        @pl.when(here.has_long(here.at(-OFFSETS[index + 1], 0)))
        def _():
            extras(lambda extra, pair, source: pltpu.make_async_copy(
                pair.at[source, :], out.at[pl.ds(PIECE + extra * GRAIN, GRAIN), :], sems.at[index, 4 + extra]).wait())


def pack(lengths, place, pairs):
    return pl.pallas_call(
        pack_kernel,
        out_shape=[jax.ShapeDtypeStruct((MESSAGE, 2 * HD), jnp.bfloat16)] * 3,
        in_specs=[SMEM, SMEM] + [HBM] * 4,
        out_specs=[HBM] * 3,
        scratch_shapes=[pltpu.SemaphoreType.DMA((3, 8))],
        name="pack",
    )(lengths, place, *pairs)


def load(source, rows, keys, values, at, sem):
    target = pl.ds(at, rows.size)
    return (
        pltpu.make_async_copy(source.at[rows, pl.ds(0, HD)], keys.at[target, :], sem),
        pltpu.make_async_copy(source.at[rows, pl.ds(HD, HD)], values.at[target, pl.ds(0, HD)], sem),
    )


def begin(copies):
    for copy in copies:
        copy.start()


def finish(copies):
    for copy in copies:
        copy.wait()


def ones_beside(values):
    values[:, HD:] = jnp.ones((values.shape[0], HD), jnp.bfloat16)


def softmax_step(peak, summed, query, keys, values, allowed=None):
    scores = lax.dot_general(
        query, keys, (((1,), (1,)), ((), ())), preferred_element_type=jnp.float32
    )
    scores = scores * SCALE
    if allowed is not None:
        scores = jnp.where(allowed, scores, LOWEST)
    top = jnp.max(scores, axis=1, keepdims=True)
    peak_new = top if peak is None else jnp.maximum(peak, top)
    weights = jnp.exp2(scores - peak_new).astype(jnp.bfloat16)
    product = jnp.dot(weights, values, preferred_element_type=jnp.float32)
    if peak is not None:
        product = summed * jnp.exp2(peak - peak_new) + product
    return peak_new, product


def stacked(queries, heads, start, count):
    return jnp.concatenate(
        [queries[pl.ds(start, count), pl.ds(head * HD, HD)] for head in heads], axis=0
    )


def own_kernel(lengths, place, queries, p0, p1, p2, p3, peak_out, summed_out, keys, values, sems):
    here = Place(place, lengths)
    pairs = (p0, p1, p2, p3)

    @pl.when(here.has_long(here.position))
    def _():
        for inner, pair in enumerate(pairs):
            start_long(
                here, here.at(0, OFFSETS[inner]), pair,
                lambda source, target: begin(
                    load(pair, source, keys, values, inner * TOK + target, sems.at[inner])),
            )
        ones_beside(values)
        for inner, pair in enumerate(pairs):
            finish(load(pair, pl.ds(0, TOK), keys, values, inner * TOK, sems.at[inner]))
        for low, high in ((0, 3), (3, 7)):
            query = stacked(queries, range(low, high), 0, TOK)
            peak, summed = softmax_step(None, None, query, keys[...], values[...])
            rows = pl.ds(low * TOK, (high - low) * TOK)
            peak_out[rows, :] = jnp.broadcast_to(peak, ((high - low) * TOK, HD))
            summed_out[rows, :] = summed


def middle_kernel(
    lengths, place, queries, b1, b2, peak_in, summed_in, peak_out, summed_out, keys, values, sems
):
    here = Place(place, lengths)

    @pl.when(here.has_long(here.position))
    def _():
        copies = []
        for index, message in enumerate((b1, b2)):
            copies.extend(load(message, pl.ds(0, PIECE), keys, values, index * PIECE, sems.at[index]))
        begin(copies)
        ones_beside(values)
        finish(copies)
        for low, high in ((0, 3), (3, 5), (5, 7)):
            query = stacked(queries, range(low, high), 0, TOK)
            rows = pl.ds(low * TOK, (high - low) * TOK)
            peak, summed = softmax_step(
                peak_in[rows, :1], summed_in[rows, :], query, keys[...], values[...])
            peak_out[rows, :] = jnp.broadcast_to(peak, ((high - low) * TOK, HD))
            summed_out[rows, :] = summed


def last_kernel(
    low, high, lengths, place, queries, p0, p1, p2, p3, b1, b2, b3, r1, r2, r3, peak_in, summed_in,
    out, keys, values, small_keys, small_values, sems, small_sems, result,
):
    here = Place(place, lengths)
    pairs, messages = (p0, p1, p2, p3), (b1, b2, b3)
    heads = range(low, high)
    count = high - low
    long_here, small_here = here.has_long(here.position), here.has_small(here.position)

    def extras(action):
        for extra in range(EXTRA):
            grain = here.start + extra
            for inner, pair in enumerate(pairs):
                @pl.when(grain // 4 == here.at(0, OFFSETS[inner]))
                def _():
                    action(load(
                        pair, rows_of(here.half(1) + grain % 4 * GRAIN, GRAIN),
                        keys, values, PIECE + extra * GRAIN, sems.at[1 + extra]))
            group = jnp.where(here.core == 0, grain // 16, grain // 4 % 4)
            for index, message in enumerate(messages):
                @pl.when(group == (here.outer + OFFSETS[index + 1] + 4) % 4)
                def _():
                    action(load(
                        message, pl.ds(PIECE + extra * GRAIN, GRAIN),
                        keys, values, PIECE + extra * GRAIN, sems.at[1 + extra]))

    def small_blocks(action):
        def block(source, row, position, slot):
            action(load(
                source, pl.ds(row, TOK), small_keys, small_values,
                pl.multiple_of(position * TOK, TOK), small_sems.at[slot]))

        @pl.when(jnp.logical_not(long_here))
        def _():
            for outer, by in enumerate(OFFSETS):
                for inner, near in enumerate(OFFSETS):
                    source = pairs[inner] if outer == 0 else messages[outer - 1]
                    block(source, 0 if outer == 0 else inner * TOK, here.at(by, near), outer * 4 + inner)

        @pl.when(long_here)
        def _():
            block(p0, 0, here.position, 0)
            away = jnp.where(here.zh == 0, -1, 1)
            for step in range(1, 1 + NEAR_BLOCKS + FAR_BLOCKS):
                position = here.position + away * step
                source, row = (r1, 0) if step == 1 else (r2, (step - 2) * TOK)
                if step > NEAR_BLOCKS:
                    source, row = r3, (step - 1 - NEAR_BLOCKS) * TOK

                @pl.when((position >= 0) & (position < 16))
                def _():
                    block(source, row, position, step)

    @pl.when(long_here)
    def _():
        begin(load(b3, pl.ds(0, PIECE), keys, values, 0, sems.at[0]))
        extras(begin)

    @pl.when(small_here)
    def _():
        small_values[:, :HD] = jnp.zeros((PLANE_TOK + SMALL, HD), jnp.bfloat16)
        small_blocks(begin)
        ones_beside(small_values)

    @pl.when(long_here)
    def _():
        ones_beside(values)
        finish(load(b3, pl.ds(0, PIECE), keys, values, 0, sems.at[0]))
        extras(finish)
        tiles = [(low, high)] if count <= 3 else [(low, low + 3), (low + 3, high)]
        for first, after in tiles:
            query = stacked(queries, range(first, after), 0, TOK)
            rows = pl.ds(first * TOK, (after - first) * TOK)
            _, summed = softmax_step(
                peak_in[rows, :1], summed_in[rows, :], query, keys[...], values[...])
            attended = (summed[:, :HD] / summed[:, HD:]).astype(jnp.bfloat16)
            for head in range(first, after):
                out[:, pl.ds((head - low) * HD, HD)] = attended[(head - first) * TOK:(head - first + 1) * TOK, :]

    @pl.when(small_here)
    def _():
        small_blocks(finish)
        column = lax.broadcasted_iota(jnp.int32, (1, SMALL), 1)

        def one_grain(grain, carry):
            at = (here.zh * 16 + here.position) * GRAINS + grain
            first, end, total = jnp.int32(0), jnp.int32(0), jnp.int32(0)
            for doc in range(DOCS):
                after = total + lengths[doc]
                inside = (total <= at) & (at < after)
                first = jnp.where(inside, total, first)
                end = jnp.where(inside, after, end)
                total = after

            @pl.when(end - first != LONG_GRAINS)
            def _():
                tokens = rows_of(grain * GRAIN, GRAIN)
                query = stacked(queries, heads, tokens.start, GRAIN)
                offset = (first - here.zh * PLANE_GRAINS) * GRAIN
                width = (end - first) * GRAIN

                def step(index, state):
                    part = rows_of(offset + index * SMALL, SMALL)
                    return softmax_step(
                        *state, query, small_keys[part, :], small_values[part, :],
                        column < width - index * SMALL)

                initial = (
                    jnp.full((count * GRAIN, 1), LOWEST, jnp.float32),
                    jnp.zeros((count * GRAIN, 2 * HD), jnp.float32),
                )
                _, summed = lax.fori_loop(0, (width + SMALL - 1) // SMALL, step, initial)
                result[...] = (summed[:, :HD] / summed[:, HD:]).astype(jnp.bfloat16)
                for index in range(count):
                    out[tokens, pl.ds(index * HD, HD)] = result[pl.ds(index * GRAIN, GRAIN), :]

            return carry

        lax.fori_loop(0, GRAINS, one_grain, 0)


def long_scratch(rows):
    return [pltpu.VMEM((rows, HD), jnp.bfloat16), pltpu.VMEM((rows, 2 * HD), jnp.bfloat16)]


STATE = [
    jax.ShapeDtypeStruct((HEADS * TOK, HD), jnp.float32),
    jax.ShapeDtypeStruct((HEADS * TOK, 2 * HD), jnp.float32),
]
PARAMS = pltpu.CompilerParams(vmem_limit_bytes=36 * 2**20)


def attend_own(lengths, place, queries, pairs):
    return pl.pallas_call(
        own_kernel,
        out_shape=STATE,
        in_specs=[SMEM, SMEM, VMEM] + [HBM] * 4,
        out_specs=[VMEM] * 2,
        scratch_shapes=long_scratch(PIECE) + [pltpu.SemaphoreType.DMA((4,))],
        compiler_params=PARAMS,
        name="own",
    )(lengths, place, queries, *pairs)


def attend_middle(lengths, place, queries, messages, state):
    return pl.pallas_call(
        middle_kernel,
        out_shape=STATE,
        in_specs=[SMEM, SMEM, VMEM] + [HBM] * 2 + [VMEM] * 2,
        out_specs=[VMEM] * 2,
        scratch_shapes=long_scratch(2 * PIECE) + [pltpu.SemaphoreType.DMA((2,))],
        input_output_aliases={5: 0, 6: 1},
        compiler_params=PARAMS,
        name="middle",
    )(lengths, place, queries, *messages, *state)


def attend_last(low, high, lengths, place, queries, pairs, messages, rings, state):
    return pl.pallas_call(
        functools.partial(last_kernel, low, high),
        out_shape=jax.ShapeDtypeStruct((TOK, (high - low) * HD), jnp.bfloat16),
        in_specs=[SMEM, SMEM, VMEM] + [HBM] * 10 + [VMEM] * 2,
        out_specs=VMEM,
        scratch_shapes=long_scratch(MESSAGE) + long_scratch(PLANE_TOK + SMALL) + [
            pltpu.SemaphoreType.DMA((1 + EXTRA,)),
            pltpu.SemaphoreType.DMA((16,)),
            pltpu.VMEM(((high - low) * GRAIN, HD), jnp.bfloat16),
        ],
        compiler_params=PARAMS,
        name="last",
    )(lengths, place, queries, *pairs, *messages, *rings, *state)


def project_kernel(group, weight, *refs):
    parts, out = refs[:4], refs[-1]
    total = refs[4][...] if len(refs) == 6 else None
    width = HEADS * HD
    for index in range(2):
        first, second = parts[2 * index], parts[2 * index + 1]
        row = pl.multiple_of(group[index] * width, HD)
        for part, offset in ((first, 0), (second, FIRST_HEADS * HD)):
            rows = pl.ds(pl.multiple_of(row + offset, HD), part.shape[1])
            term = jnp.dot(part[...], weight[rows, :], preferred_element_type=jnp.float32)
            total = term if total is None else total + term
    out[...] = total.astype(out.dtype)


def project(groups, weight, parts, before, dtype):
    return pl.pallas_call(
        project_kernel,
        out_shape=jax.ShapeDtypeStruct((TOK, weight.shape[1]), dtype),
        in_specs=[SMEM] + [VMEM] * (1 + len(parts) + len(before)),
        out_specs=VMEM,
        compiler_params=pltpu.CompilerParams(vmem_limit_bytes=24 * 2**20),
        name="project",
    )(groups, weight, *parts, *before)


def far_reach(lengths):
    ends = jnp.cumsum(lengths)
    starts = ends - lengths
    start = jnp.sum(jnp.where(lengths == LONG_GRAINS, starts, 0))
    end = start + LONG_GRAINS
    first, after = start - start % 4, end + (-end) % 4
    before_it = jnp.sum(jnp.where((starts <= first) & (first < ends), first - starts, 0))
    behind_it = jnp.sum(jnp.where((starts < after) & (after <= ends), ends - after, 0))
    before_it = jnp.where(start % 4 == 0, 0, before_it)
    behind_it = jnp.where(end % 4 == 0, 0, behind_it)
    return jnp.maximum(before_it, behind_it) > NEAR_BLOCKS * 4


def per_device(queries, keys, values, doc_lengths, out_weight):
    zh, y, x, zl, c = (lax.axis_index(a) for a in ("zh", "y", "x", "zl", "c"))
    place = jnp.stack([zh, y, x, c]).astype(jnp.int32)
    own = jnp.concatenate([keys, values], axis=1)
    pair = jnp.concatenate([own, swap(own, "zh")], axis=0)
    one = ring(own, 1)
    two = ring(jnp.concatenate([own, one], axis=0), 2)

    def fetch(block):
        def step(index, carry):
            block, blocks = carry
            block = ring(block, 1)
            return block, lax.dynamic_update_slice_in_dim(blocks, block, index * TOK, 0)

        return lax.fori_loop(
            0, FAR_BLOCKS, step, (block, jnp.zeros((FAR_BLOCKS * TOK, 2 * HD), jnp.bfloat16)))[1]

    far = lax.cond(
        far_reach(doc_lengths), fetch,
        lambda block: jnp.zeros((FAR_BLOCKS * TOK, 2 * HD), jnp.bfloat16), two[TOK:])
    pairs = [pair] + [move(pair, 0, -k) for k in OFFSETS[1:]]
    sent = pack(doc_lengths, place, pairs)
    messages = [move(block, -k, 0) for block, k in zip(sent, OFFSETS[1:])]
    state = attend_own(doc_lengths, place, queries, pairs)
    state = attend_middle(doc_lengths, place, queries, messages[:2], state)
    halves = []
    for low, high in ((0, FIRST_HEADS), (FIRST_HEADS, HEADS)):
        halves.append(attend_last(
            low, high, doc_lengths, place, queries, pairs, messages, (one, two, far), state))
    across = [swap(part, "zl") for part in halves]
    beside = [swap(part, "c") for part in halves]
    beyond = [swap(part, "c") for part in across]
    group = (zl * 2 + c).astype(jnp.int32)
    near = project(jnp.stack([group, group ^ 1]), out_weight, halves + beside, [], jnp.float32)
    return project(
        jnp.stack([group ^ 2, group ^ 3]), out_weight, across + beyond, [near], jnp.bfloat16)


def solution(mesh):
    fine = Mesh(np.asarray(mesh.devices).reshape(2, 4, 4, 2, 2), ("zh", "y", "x", "zl", "c"))
    seq, kv = ("zh", "y", "x"), ("zl", "c")
    return jax.shard_map(
        per_device,
        mesh=fine,
        in_specs=(P(seq, kv), P(seq, kv), P(seq, kv), P(), P(None, kv)),
        out_specs=P(seq, kv),
        check_vma=False,
    )
```

```python
import functools

import jax
import jax.numpy as jnp
import numpy as np
from jax import lax
from jax.experimental import pallas as pl
from jax.experimental.pallas import tpu as pltpu
from jax.sharding import Mesh, PartitionSpec as P

HD = 128
GRAIN = 64
TOK = 256
HEADS = 7
GRAINS = TOK // GRAIN
DOCS = 16
LONG_GRAINS = 68
PLANE_GRAINS = 64
PLANE_TOK = PLANE_GRAINS * GRAIN
EXTRA = LONG_GRAINS - PLANE_GRAINS
PIECE = 4 * TOK
MESSAGE = PIECE + EXTRA * GRAIN
SMALL = 256
NEAR_BLOCKS = 3
FAR_BLOCKS = 9
CHUNKS = ((0, 4), (4, 7))
TILE = 896
FLAG = HEADS * TOK
SCALE = 1.4426950408889634 / HD**0.5
LOWEST = -1e30
SAFE = (90.0 / SCALE) ** 2
UNSAFE = 1e30
OFFSETS = (0, -1, 1, 2)

SMEM = pl.BlockSpec(memory_space=pltpu.SMEM)
VMEM = pl.BlockSpec(memory_space=pltpu.VMEM)
HBM = pl.BlockSpec(memory_space=pltpu.HBM)


def turn(by_first, by_second):
    pairs = []
    for y in range(4):
        for x in range(4):
            pairs.append((y, x, 0, (y + by_first) % 4, (x + by_second) % 4))
            pairs.append((y, x, 1, (y + by_second) % 4, (x + by_first) % 4))
    return [((y * 4 + x) * 2 + c, (to_y * 4 + to_x) * 2 + c) for y, x, c, to_y, to_x in pairs]


def move(block, by_first, by_second):
    return lax.ppermute(block, ("y", "x", "c"), turn(by_first, by_second))


def ring(block, step):
    pairs = []
    for at in range(16):
        pairs.append((at, (at + step) % 16))
        pairs.append((16 + at, 16 + (at - step) % 16))
    return lax.ppermute(block, ("zh", "y", "x"), pairs)


def swap(block, axis):
    return lax.ppermute(block, axis, [(0, 1), (1, 0)])


class Lengths:
    def __init__(self, table):
        self.table = table

    def __getitem__(self, doc):
        return self.table[4 + doc]


class Place:
    def __init__(self, table):
        lengths = Lengths(table)
        self.zh, y, x, self.core = table[0], table[1], table[2], table[3]
        self.inner = jnp.where(self.core == 0, x, y)
        self.outer = jnp.where(self.core == 0, y, x)
        self.position = y * 4 + x
        total, start = jnp.int32(0), jnp.int32(0)
        for doc in range(DOCS):
            start = jnp.where(lengths[doc] == LONG_GRAINS, total, start)
            total = total + lengths[doc]
        self.start, self.stop = start, start + EXTRA

    def at(self, outer_by, inner_by):
        outer, inner = (self.outer + outer_by + 4) % 4, (self.inner + inner_by + 4) % 4
        return jnp.where(self.core == 0, outer * 4 + inner, inner * 4 + outer)

    def has_long(self, position):
        return jnp.where(self.zh == 0, position * 4 + 3 >= self.start, position * 4 < self.stop)

    def has_small(self, position):
        return jnp.where(self.zh == 0, position * 4 < self.start, position * 4 + 3 >= self.stop)


def rows_of(start, count):
    return pl.ds(pl.multiple_of(start, GRAIN), count)


def bounds(lengths, grain):
    first, end, total = jnp.int32(0), jnp.int32(0), jnp.int32(0)
    for doc in range(DOCS):
        after = total + lengths[doc]
        inside = (total <= grain) & (grain < after)
        first = jnp.where(inside, total, first)
        end = jnp.where(inside, after, end)
        total = after
    return first, end


def join_kernel(keys, values, out, sems):
    copies = [
        pltpu.make_async_copy(keys, out.at[:, pl.ds(0, HD)], sems.at[0]),
        pltpu.make_async_copy(values, out.at[:, pl.ds(HD, HD)], sems.at[1]),
    ]
    for copy in copies:
        copy.start()
    for copy in copies:
        copy.wait()


def join(keys, values):
    return pl.pallas_call(
        join_kernel,
        out_shape=jax.ShapeDtypeStruct((TOK, 2 * HD), jnp.bfloat16),
        in_specs=[HBM, HBM],
        out_specs=VMEM,
        scratch_shapes=[pltpu.SemaphoreType.DMA((2,))],
        name="join",
    )(keys, values)


def pack_kernel(table, *refs):
    natives, others, (own, m1, m2, m3, far) = refs[:4], refs[4:8], refs[-5:]
    here = Place(table)
    for inner in range(4):
        cut = jnp.clip(here.start - here.at(0, OFFSETS[inner]) * 4, 0, 4)
        for plane, blocks in ((here.zh, natives), (1 - here.zh, others)):
            @pl.when(cut == 4 * plane)
            def _():
                own[pl.ds(inner * TOK, TOK), :] = blocks[inner][...]

            @pl.when((cut > 0) & (cut < 4))
            def _():
                for grain in range(GRAINS):
                    @pl.when((grain < cut).astype(jnp.int32) == plane)
                    def _():
                        own[pl.ds(inner * TOK + grain * GRAIN, GRAIN), :] = blocks[inner][
                            pl.ds(grain * GRAIN, GRAIN), :]

    for extra in range(EXTRA):
        grain = here.start + extra
        for inner in range(4):
            for plane, blocks in ((1, natives), (0, others)):
                @pl.when((grain // 4 == here.at(0, OFFSETS[inner])) & (here.zh == plane))
                def _():
                    own[pl.ds(PIECE + extra * GRAIN, GRAIN), :] = blocks[inner][
                        rows_of(grain % 4 * GRAIN, GRAIN), :]

    for index, out in enumerate((m1, m2, m3)):
        to_long = here.has_long(here.at(-OFFSETS[index + 1], 0))

        @pl.when(to_long)
        def _():
            out[...] = own[...]

        @pl.when(jnp.logical_not(to_long))
        def _():
            for inner in range(4):
                out[pl.ds(inner * TOK, TOK), :] = natives[inner][...]

    lengths = Lengths(table)
    start, end = here.start, here.start + LONG_GRAINS
    before, after = start - start % 4, end + (4 - end % 4) % 4
    reach_before = jnp.where(start % 4 == 0, 0, before - bounds(lengths, before)[0])
    reach_after = jnp.where(end % 4 == 0, 0, bounds(lengths, after - 1)[1] - after)
    far[0] = (jnp.maximum(reach_before, reach_after) > NEAR_BLOCKS * 4).astype(jnp.int32)


def pack(table, natives, others, after):
    return pl.pallas_call(
        pack_kernel,
        out_shape=[jax.ShapeDtypeStruct((MESSAGE, 2 * HD), jnp.bfloat16)] * 4 + [
            jax.ShapeDtypeStruct((1,), jnp.int32)],
        in_specs=[SMEM] + [VMEM] * 8 + [HBM] * len(after),
        out_specs=[VMEM] * 4 + [SMEM],
        compiler_params=PARAMS,
        name="pack",
    )(table, *natives, *others, *after)


def put(block, keys, values, rows):
    keys[rows, :] = block[:, :HD]
    values[rows, :HD] = block[:, HD:]


def ones_beside(values):
    values[:, HD:] = jnp.ones((values.shape[0], HD), jnp.bfloat16)


def largest_square(block):
    block = block.astype(jnp.float32)
    return jnp.max(jnp.sum(block * block, axis=1, keepdims=True))


def plain_step(summed, query, keys, values):
    scores = lax.dot_general(
        query, keys, (((1,), (1,)), ((), ())), preferred_element_type=jnp.float32
    )
    weights = jnp.exp2(scores * SCALE).astype(jnp.bfloat16)
    product = jnp.dot(weights, values, preferred_element_type=jnp.float32)
    return product if summed is None else summed + product


def softmax_step(peak, summed, query, keys, values, allowed=None):
    scores = lax.dot_general(
        query, keys, (((1,), (1,)), ((), ())), preferred_element_type=jnp.float32
    )
    scores = scores * SCALE
    if allowed is not None:
        scores = jnp.where(allowed, scores, LOWEST)
    top = jnp.max(scores, axis=1, keepdims=True)
    peak_new = top if peak is None else jnp.maximum(peak, top)
    weights = jnp.exp2(scores - peak_new).astype(jnp.bfloat16)
    product = jnp.dot(weights, values, preferred_element_type=jnp.float32)
    if peak is not None:
        product = summed * jnp.exp2(peak - peak_new) + product
    return peak_new, product


def stacked(queries, heads, start, count):
    return jnp.concatenate(
        [queries[pl.ds(start, count), pl.ds(head * HD, HD)] for head in heads], axis=0
    )


def own_kernel(table, queries, own, rows_out, peak_out, summed_out, keys, values):
    here = Place(table)

    @pl.when(here.has_long(here.position))
    def _():
        for head in range(HEADS):
            rows_out[pl.ds(head * TOK, TOK), :] = queries[:, pl.ds(head * HD, HD)]
        ones_beside(values)
        put(own[pl.ds(0, PIECE), :], keys, values, pl.ds(0, PIECE))
        queries_square = largest_square(rows_out[...])
        plain = queries_square * largest_square(keys[...]) <= SAFE
        peak_out[pl.ds(FLAG, 8), :] = jnp.full((8, HD), jnp.where(plain, queries_square, UNSAFE))

        @pl.when(plain)
        def _():
            peak_out[pl.ds(0, FLAG), :] = jnp.zeros((FLAG, HD), jnp.float32)

            def tile(index, carry):
                rows = pl.ds(pl.multiple_of(index * TILE, TILE), TILE)
                summed_out[rows, :] = plain_step(None, rows_out[rows, :], keys[...], values[...])
                return carry

            lax.fori_loop(0, FLAG // TILE, tile, 0)

        @pl.when(jnp.logical_not(plain))
        def _():
            def tile(index, carry):
                rows = pl.ds(pl.multiple_of(index * TOK, TOK), TOK)
                peak, summed = softmax_step(None, None, rows_out[rows, :], keys[...], values[...])
                peak_out[rows, :] = jnp.broadcast_to(peak, (TOK, HD))
                summed_out[rows, :] = summed
                return carry

            lax.fori_loop(0, HEADS, tile, 0)


def still_plain(peak, keys):
    return jnp.max(peak[pl.ds(FLAG, 8), :]) * largest_square(keys[...]) <= SAFE


def middle_kernel(
    table, queries, b1, b2, peak_in, summed_in, peak_out, summed_out, keys, values
):
    here = Place(table)

    @pl.when(here.has_long(here.position))
    def _():
        ones_beside(values)
        for index, message in enumerate((b1, b2)):
            put(message[pl.ds(0, PIECE), :], keys, values, pl.ds(index * PIECE, PIECE))
        plain = still_plain(peak_in, keys)

        @pl.when(plain)
        def _():
            def tile(index, carry):
                rows = pl.ds(pl.multiple_of(index * TILE, TILE), TILE)
                query, summed = queries[rows, :], summed_in[rows, :]
                for part in (pl.ds(0, PIECE), pl.ds(PIECE, PIECE)):
                    summed = plain_step(summed, query, keys[part, :], values[part, :])
                summed_out[rows, :] = summed
                return carry

            lax.fori_loop(0, FLAG // TILE, tile, 0)

        @pl.when(jnp.logical_not(plain))
        def _():
            def tile(index, carry):
                rows = pl.ds(pl.multiple_of(index * TOK, TOK), TOK)
                peak, summed = softmax_step(
                    peak_in[rows, :1], summed_in[rows, :], queries[rows, :], keys[...], values[...])
                peak_out[rows, :] = jnp.broadcast_to(peak, (TOK, HD))
                summed_out[rows, :] = summed
                return carry

            lax.fori_loop(0, HEADS, tile, 0)
            peak_out[pl.ds(FLAG, 8), :] = jnp.full((8, HD), UNSAFE, jnp.float32)


def last_kernel(low, high, table, rows_in, own, b1, b2, b3, small, peak_in, summed_in, *refs):
    here = Place(table)
    count = high - low
    if low == 0:
        queries, n0, n1, n2, n3, out, rest, keys, values, result, held, *small_scratch = refs
        pure = jnp.logical_not(here.has_long(here.position))

        @pl.when(jnp.logical_not(pure))
        def _():
            held[...] = small[...]

        small_kernel(
            False, table, queries, n0, n1, n2, n3, b1, b2, b3, held, *small_scratch)
        small = held
        rest[...] = held[:, pl.ds(high * HD, (HEADS - high) * HD)]
    else:
        out, keys, values, result = refs[-4:]

    @pl.when(here.has_long(here.position))
    def _():
        ones_beside(values)
        put(b3[pl.ds(0, PIECE), :], keys, values, pl.ds(0, PIECE))
        for extra in range(EXTRA):
            grain = here.start + extra
            rows = pl.ds(PIECE + extra * GRAIN, GRAIN)
            group = jnp.where(here.core == 0, grain // 16, grain // 4 % 4)
            for message, by in zip((own, b1, b2, b3), OFFSETS):
                @pl.when(group == (here.outer + by + 4) % 4)
                def _():
                    put(message[rows, :], keys, values, rows)

        plain = still_plain(peak_in, keys)

        @pl.when(plain)
        def _():
            rows = pl.ds(low * TOK, count * TOK)
            summed = plain_step(summed_in[rows, :], rows_in[rows, :], keys[...], values[...])
            result[...] = (summed[:, :HD] / summed[:, HD:]).astype(jnp.bfloat16)

        @pl.when(jnp.logical_not(plain))
        def _():
            def tile(index, carry):
                rows = pl.ds(pl.multiple_of((low + index) * TOK, TOK), TOK)
                _, summed = softmax_step(
                    peak_in[rows, :1], summed_in[rows, :], rows_in[rows, :], keys[...], values[...])
                result[pl.ds(pl.multiple_of(index * TOK, TOK), TOK), :] = (
                    summed[:, :HD] / summed[:, HD:]).astype(jnp.bfloat16)
                return carry

            lax.fori_loop(0, count, tile, 0)

        for index in range(count):
            out[:, pl.ds(index * HD, HD)] = result[pl.ds(index * TOK, TOK), :]

    for grain in range(GRAINS):
        at = here.position * GRAINS + grain
        tokens = pl.ds(grain * GRAIN, GRAIN)

        @pl.when(jnp.where(here.zh == 0, at < here.start, at >= here.stop))
        def _():
            columns = pl.ds(0, count * HD)
            out[tokens, :] = small[tokens, columns]


def small_kernel(straddle, table, *refs):
    if straddle:
        far, queries, n0, r1, r2, r3, r4, _, out = refs[:9]
    else:
        queries, n0, n1, n2, n3, b1, b2, b3, out = refs[:9]
    keys, values, result = refs[-3:]
    here, lengths = Place(table), Lengths(table)
    long_here, small_here = here.has_long(here.position), here.has_small(here.position)

    @pl.when(small_here & (long_here if straddle else jnp.logical_not(long_here)))
    def _():
        def block(source, row, position):
            put(source[pl.ds(row, TOK), :], keys, values, rows_of(position * TOK, TOK))

        ones_beside(values)
        if straddle:
            values[:, :HD] = jnp.zeros((PLANE_TOK + SMALL, HD), jnp.bfloat16)
            block(n0, 0, here.position)
            away = jnp.where(here.zh == 0, -1, 1)
            for step in range(1, 1 + NEAR_BLOCKS + FAR_BLOCKS):
                position = here.position + away * step
                inside = (position >= 0) & (position < 16)
                source, row = ((r1, r2, r3)[step - 1], 0) if step <= NEAR_BLOCKS else (
                    r4, (step - 1 - NEAR_BLOCKS) * TOK)
                if step > NEAR_BLOCKS:
                    inside = inside & (far[0] == 1)

                @pl.when(inside)
                def _():
                    block(source, row, position)
        else:
            values[pl.ds(PLANE_TOK, SMALL), :HD] = jnp.zeros((SMALL, HD), jnp.bfloat16)
            for inner, near in enumerate(OFFSETS):
                block((n0, n1, n2, n3)[inner], 0, here.at(0, near))
                for message, by in zip((b1, b2, b3), OFFSETS[1:]):
                    block(message, inner * TOK, here.at(by, near))

        column = lax.broadcasted_iota(jnp.int32, (1, SMALL), 1)

        def one_grain(grain, carry):
            first, end = bounds(lengths, (here.zh * 16 + here.position) * GRAINS + grain)

            @pl.when(end - first != LONG_GRAINS)
            def _():
                tokens = rows_of(grain * GRAIN, GRAIN)
                query = stacked(queries, range(HEADS), tokens.start, GRAIN)
                offset = (first - here.zh * PLANE_GRAINS) * GRAIN
                width = (end - first) * GRAIN

                def step(index, state):
                    part = rows_of(offset + index * SMALL, SMALL)
                    return softmax_step(
                        *state, query, keys[part, :], values[part, :],
                        column < width - index * SMALL)

                initial = (
                    jnp.full((HEADS * GRAIN, 1), LOWEST, jnp.float32),
                    jnp.zeros((HEADS * GRAIN, 2 * HD), jnp.float32),
                )
                _, summed = lax.fori_loop(0, (width + SMALL - 1) // SMALL, step, initial)
                result[...] = (summed[:, :HD] / summed[:, HD:]).astype(jnp.bfloat16)
                for head in range(HEADS):
                    out[tokens, pl.ds(head * HD, HD)] = result[pl.ds(head * GRAIN, GRAIN), :]

            return carry

        lax.fori_loop(0, GRAINS, one_grain, 0)


def scratch(rows):
    return [pltpu.VMEM((rows, HD), jnp.bfloat16), pltpu.VMEM((rows, 2 * HD), jnp.bfloat16)]


def cost(keys, heads=HEADS):
    rows = heads * TOK
    return pl.CostEstimate(
        flops=6 * rows * keys * HD, bytes_accessed=rows * HD * 4, transcendentals=rows * keys)


STATE = [
    jax.ShapeDtypeStruct((FLAG + 8, HD), jnp.float32),
    jax.ShapeDtypeStruct((HEADS * TOK, 2 * HD), jnp.float32),
]
PARAMS = pltpu.CompilerParams(vmem_limit_bytes=28 * 2**20)


def attend_own(table, queries, own):
    rows = jax.ShapeDtypeStruct((HEADS * TOK, HD), jnp.bfloat16)
    return pl.pallas_call(
        own_kernel,
        out_shape=[rows] + STATE,
        in_specs=[SMEM, VMEM, VMEM],
        out_specs=[VMEM] * 3,
        scratch_shapes=scratch(PIECE),
        compiler_params=PARAMS,
        cost_estimate=cost(PIECE),
        name="own",
    )(table, queries, own)


def attend_middle(table, rows, messages, state, weight, after):
    def kernel(*refs):
        middle_kernel(*refs[:6], *refs[8:])

    return pl.pallas_call(
        kernel,
        out_shape=STATE,
        in_specs=[SMEM] + [VMEM] * 6 + [HBM],
        out_specs=[VMEM] * 2,
        scratch_shapes=scratch(2 * PIECE),
        input_output_aliases={4: 0, 5: 1},
        compiler_params=PARAMS,
        cost_estimate=cost(2 * PIECE),
        name="middle",
    )(table, rows, *messages, *state, weight, after)


def attend_last(low, high, table, blocks, more):
    shapes = [jax.ShapeDtypeStruct((TOK, (high - low) * HD), jnp.bfloat16)]
    scratches = scratch(MESSAGE) + [pltpu.VMEM(((high - low) * TOK, HD), jnp.bfloat16)]
    if low == 0:
        shapes.append(jax.ShapeDtypeStruct((TOK, (HEADS - high) * HD), jnp.bfloat16))
        scratches += [pltpu.VMEM((TOK, HEADS * HD), jnp.bfloat16)] + scratch(PLANE_TOK + SMALL) + [
            pltpu.VMEM((HEADS * GRAIN, HD), jnp.bfloat16)]
    return pl.pallas_call(
        functools.partial(last_kernel, low, high),
        out_shape=shapes,
        in_specs=[SMEM] + [VMEM] * (len(blocks) + len(more)),
        out_specs=[VMEM] * len(shapes),
        scratch_shapes=scratches,
        compiler_params=PARAMS,
        cost_estimate=cost(MESSAGE, high - low),
        name="last",
    )(table, *blocks, *more)


def attend_small(scalars, blocks):
    return pl.pallas_call(
        functools.partial(small_kernel, True),
        out_shape=jax.ShapeDtypeStruct((TOK, HEADS * HD), jnp.bfloat16),
        in_specs=[SMEM] * len(scalars) + [VMEM] * len(blocks),
        out_specs=VMEM,
        scratch_shapes=scratch(PLANE_TOK + SMALL) + [pltpu.VMEM((HEADS * GRAIN, HD), jnp.bfloat16)],
        compiler_params=PARAMS,
        cost_estimate=cost(TOK),
        name="small",
    )(*scalars, *blocks)


def add_products(total, groups, weight, parts):
    for index, head, part in parts:
        rows = pl.ds(pl.multiple_of(groups[index] * HEADS * HD + head * HD, HD), part.shape[1])
        term = jnp.dot(part[...], weight[rows, :], preferred_element_type=jnp.float32)
        total = term if total is None else total + term
    return total


def project_kernel(where, groups, weight, *refs):
    parts, before, out = refs[:len(where)], refs[len(where):-1], refs[-1]
    total = before[0][...] if before else None
    total = add_products(total, groups, weight, [(*w, p) for w, p in zip(where, parts)])
    out[...] = total.astype(out.dtype)


def project(where, groups, weight, parts, before, dtype):
    depth = sum(part.shape[1] for part in parts)
    return pl.pallas_call(
        functools.partial(project_kernel, where),
        out_shape=jax.ShapeDtypeStruct((TOK, weight.shape[1]), dtype),
        in_specs=[SMEM] + [VMEM] * (1 + len(parts) + len(before)),
        out_specs=VMEM,
        compiler_params=pltpu.CompilerParams(vmem_limit_bytes=20 * 2**20),
        cost_estimate=pl.CostEstimate(
            flops=2 * TOK * depth * weight.shape[1], bytes_accessed=2 * depth * weight.shape[1],
            transcendentals=0),
        name="project",
    )(groups, weight, *parts, *before)


def per_device(queries, keys, values, doc_lengths, out_weight):
    zh, y, x, zl, c = (lax.axis_index(a) for a in ("zh", "y", "x", "zl", "c"))
    table = jnp.concatenate([jnp.stack([zh, y, x, c]).astype(jnp.int32), doc_lengths])
    native = join(keys, values)
    other = swap(native, "zh")
    natives = [native] + [move(native, 0, -k) for k in OFFSETS[1:]]
    others = [other] + [move(other, 0, -k) for k in OFFSETS[1:]]
    rings = [ring(native, step) for step in range(1, 1 + NEAR_BLOCKS)]
    own, *sent, is_far = pack(table, natives, others, rings)
    messages = [move(block, -k, 0) for block, k in zip(sent, OFFSETS[1:])]
    nothing = jnp.zeros((FAR_BLOCKS * TOK, 2 * HD), jnp.bfloat16)

    def fetch(block):
        def step(index, carry):
            block, blocks = carry
            block = ring(block, 1)
            at = jnp.maximum(index - NEAR_BLOCKS, 0) * TOK
            return block, lax.dynamic_update_slice_in_dim(blocks, block, at, 0)

        return lax.fori_loop(0, NEAR_BLOCKS + FAR_BLOCKS, step, (block, nothing))[1]

    beyond_rings = lax.cond(is_far[0] == 1, fetch, lambda block: nothing, native)
    rows, *state = attend_own(table, queries, own)
    small = attend_small((table, is_far), (queries, native, *rings, beyond_rings, rows))
    state = attend_middle(table, rows, messages[:2], state, out_weight, small)
    (first, middle), (second, _) = CHUNKS
    some, rest = attend_last(
        first, middle, table, (rows, own, *messages, small, *state), (queries, *natives))
    chunks = [some] + list(attend_last(
        second, HEADS, table, (rows, own, *messages, rest, *state), ()))
    across = [swap(part, "zl") for part in chunks]
    beside = [swap(part, "c") for part in chunks]
    group = (zl * 2 + c).astype(jnp.int32)
    groups = jnp.stack([group, group ^ 1, group ^ 2, group ^ 3])
    mixed = project(
        [(0, first), (0, second), (1, first), (1, second)], groups, out_weight, chunks + beside, [],
        jnp.float32)
    across, mixed = lax.optimization_barrier((across, mixed))
    beyond = [swap(part, "c") for part in across]
    mixed = project(
        [(2, first), (3, first)], groups, out_weight, [across[0], beyond[0]], [mixed], jnp.float32)
    return project(
        [(2, second), (3, second)], groups, out_weight, [across[1], beyond[1]], [mixed],
        jnp.bfloat16)


def solution(mesh):
    fine = Mesh(np.asarray(mesh.devices).reshape(2, 4, 4, 2, 2), ("zh", "y", "x", "zl", "c"))
    seq, kv = ("zh", "y", "x"), ("zl", "c")
    return jax.shard_map(
        per_device,
        mesh=fine,
        in_specs=(P(seq, kv), P(seq, kv), P(seq, kv), P(), P(None, kv)),
        out_specs=P(seq, kv),
        check_vma=False,
    )
```

```python
import functools

import jax
import jax.numpy as jnp
import numpy as np
from jax import lax
from jax.experimental import pallas as pl
from jax.experimental.pallas import tpu as pltpu
from jax.sharding import Mesh, PartitionSpec as P

HD = 128
GRAIN = 64
TOK = 256
HEADS = 7
GRAINS = TOK // GRAIN
DOCS = 16
LONG_GRAINS = 68
PLANE_GRAINS = 64
PLANE_TOK = PLANE_GRAINS * GRAIN
EXTRA = LONG_GRAINS - PLANE_GRAINS
PIECE = 4 * TOK
MESSAGE = PIECE + EXTRA * GRAIN
SMALL = 256
NEAR_BLOCKS = 3
FAR_BLOCKS = 9
CHUNKS = ((0, 4), (4, 7))
TILE = 896
FLAG = HEADS * TOK
SCALE = 1.4426950408889634 / HD**0.5
LOWEST = -1e30
SAFE = (90.0 / SCALE) ** 2
UNSAFE = 1e30
OFFSETS = (0, -1, 1, 2)

SMEM = pl.BlockSpec(memory_space=pltpu.SMEM)
VMEM = pl.BlockSpec(memory_space=pltpu.VMEM)
HBM = pl.BlockSpec(memory_space=pltpu.HBM)


def turn(by_first, by_second):
    pairs = []
    for y in range(4):
        for x in range(4):
            pairs.append((y, x, 0, (y + by_first) % 4, (x + by_second) % 4))
            pairs.append((y, x, 1, (y + by_second) % 4, (x + by_first) % 4))
    return [((y * 4 + x) * 2 + c, (to_y * 4 + to_x) * 2 + c) for y, x, c, to_y, to_x in pairs]


def move(block, by_first, by_second):
    return lax.ppermute(block, ("y", "x", "c"), turn(by_first, by_second))


def ring(block, step):
    pairs = []
    for at in range(16):
        pairs.append((at, (at + step) % 16))
        pairs.append((16 + at, 16 + (at - step) % 16))
    return lax.ppermute(block, ("zh", "y", "x"), pairs)


def swap(block, axis):
    return lax.ppermute(block, axis, [(0, 1), (1, 0)])


class Lengths:
    def __init__(self, table):
        self.table = table

    def __getitem__(self, doc):
        return self.table[4 + doc]


class Place:
    def __init__(self, table):
        lengths = Lengths(table)
        self.zh, y, x, self.core = table[0], table[1], table[2], table[3]
        self.inner = jnp.where(self.core == 0, x, y)
        self.outer = jnp.where(self.core == 0, y, x)
        self.position = y * 4 + x
        total, start = jnp.int32(0), jnp.int32(0)
        for doc in range(DOCS):
            start = jnp.where(lengths[doc] == LONG_GRAINS, total, start)
            total = total + lengths[doc]
        self.start, self.stop = start, start + EXTRA

    def at(self, outer_by, inner_by):
        outer, inner = (self.outer + outer_by + 4) % 4, (self.inner + inner_by + 4) % 4
        return jnp.where(self.core == 0, outer * 4 + inner, inner * 4 + outer)

    def has_long(self, position):
        return jnp.where(self.zh == 0, position * 4 + 3 >= self.start, position * 4 < self.stop)

    def has_small(self, position):
        return jnp.where(self.zh == 0, position * 4 < self.start, position * 4 + 3 >= self.stop)


def rows_of(start, count):
    return pl.ds(pl.multiple_of(start, GRAIN), count)


def bounds(lengths, grain):
    first, end, total = jnp.int32(0), jnp.int32(0), jnp.int32(0)
    for doc in range(DOCS):
        after = total + lengths[doc]
        inside = (total <= grain) & (grain < after)
        first = jnp.where(inside, total, first)
        end = jnp.where(inside, after, end)
        total = after
    return first, end


def join_kernel(keys, values, out, sems):
    copies = [
        pltpu.make_async_copy(keys, out.at[:, pl.ds(0, HD)], sems.at[0]),
        pltpu.make_async_copy(values, out.at[:, pl.ds(HD, HD)], sems.at[1]),
    ]
    for copy in copies:
        copy.start()
    for copy in copies:
        copy.wait()


def join(keys, values):
    return pl.pallas_call(
        join_kernel,
        out_shape=jax.ShapeDtypeStruct((TOK, 2 * HD), jnp.bfloat16),
        in_specs=[HBM, HBM],
        out_specs=VMEM,
        scratch_shapes=[pltpu.SemaphoreType.DMA((2,))],
        name="join",
    )(keys, values)


def pack_kernel(table, *refs):
    natives, others, (own, m1, m2, m3, far) = refs[:4], refs[4:8], refs[-5:]
    here = Place(table)
    for inner in range(4):
        cut = jnp.clip(here.start - here.at(0, OFFSETS[inner]) * 4, 0, 4)
        for plane, blocks in ((here.zh, natives), (1 - here.zh, others)):
            @pl.when(cut == 4 * plane)
            def _():
                own[pl.ds(inner * TOK, TOK), :] = blocks[inner][...]

            @pl.when((cut > 0) & (cut < 4))
            def _():
                for grain in range(GRAINS):
                    @pl.when((grain < cut).astype(jnp.int32) == plane)
                    def _():
                        own[pl.ds(inner * TOK + grain * GRAIN, GRAIN), :] = blocks[inner][
                            pl.ds(grain * GRAIN, GRAIN), :]

    for extra in range(EXTRA):
        grain = here.start + extra
        for inner in range(4):
            for plane, blocks in ((1, natives), (0, others)):
                @pl.when((grain // 4 == here.at(0, OFFSETS[inner])) & (here.zh == plane))
                def _():
                    own[pl.ds(PIECE + extra * GRAIN, GRAIN), :] = blocks[inner][
                        rows_of(grain % 4 * GRAIN, GRAIN), :]

    for index, out in enumerate((m1, m2, m3)):
        to_long = here.has_long(here.at(-OFFSETS[index + 1], 0))

        @pl.when(to_long)
        def _():
            out[...] = own[...]

        @pl.when(jnp.logical_not(to_long))
        def _():
            for inner in range(4):
                out[pl.ds(inner * TOK, TOK), :] = natives[inner][...]

    lengths = Lengths(table)
    start, end = here.start, here.start + LONG_GRAINS
    before, after = start - start % 4, end + (4 - end % 4) % 4
    reach_before = jnp.where(start % 4 == 0, 0, before - bounds(lengths, before)[0])
    reach_after = jnp.where(end % 4 == 0, 0, bounds(lengths, after - 1)[1] - after)
    far[0] = (jnp.maximum(reach_before, reach_after) > NEAR_BLOCKS * 4).astype(jnp.int32)


def pack(table, natives, others, after):
    return pl.pallas_call(
        pack_kernel,
        out_shape=[jax.ShapeDtypeStruct((MESSAGE, 2 * HD), jnp.bfloat16)] * 4 + [
            jax.ShapeDtypeStruct((1,), jnp.int32)],
        in_specs=[SMEM] + [VMEM] * 8 + [HBM] * len(after),
        out_specs=[VMEM] * 4 + [SMEM],
        compiler_params=PARAMS,
        name="pack",
    )(table, *natives, *others, *after)


def put(block, keys, values, rows):
    keys[rows, :] = block[:, :HD]
    values[rows, :HD] = block[:, HD:]


def ones_beside(values):
    values[:, HD:] = jnp.ones((values.shape[0], HD), jnp.bfloat16)


def largest_square(block):
    block = block.astype(jnp.float32)
    return jnp.max(jnp.sum(block * block, axis=1, keepdims=True))


def plain_step(summed, query, keys, values):
    scores = lax.dot_general(
        query, keys, (((1,), (1,)), ((), ())), preferred_element_type=jnp.float32
    )
    weights = jnp.exp2(scores * SCALE).astype(jnp.bfloat16)
    product = jnp.dot(weights, values, preferred_element_type=jnp.float32)
    return product if summed is None else summed + product


def softmax_step(peak, summed, query, keys, values, allowed=None):
    scores = lax.dot_general(
        query, keys, (((1,), (1,)), ((), ())), preferred_element_type=jnp.float32
    )
    scores = scores * SCALE
    if allowed is not None:
        scores = jnp.where(allowed, scores, LOWEST)
    top = jnp.max(scores, axis=1, keepdims=True)
    peak_new = top if peak is None else jnp.maximum(peak, top)
    weights = jnp.exp2(scores - peak_new).astype(jnp.bfloat16)
    product = jnp.dot(weights, values, preferred_element_type=jnp.float32)
    if peak is not None:
        product = summed * jnp.exp2(peak - peak_new) + product
    return peak_new, product


def stacked(queries, heads, start, count):
    return jnp.concatenate(
        [queries[pl.ds(start, count), pl.ds(head * HD, HD)] for head in heads], axis=0
    )


def own_kernel(table, queries, own, rows_out, peak_out, summed_out, keys, values):
    here = Place(table)

    @pl.when(here.has_long(here.position))
    def _():
        for head in range(HEADS):
            rows_out[pl.ds(head * TOK, TOK), :] = queries[:, pl.ds(head * HD, HD)]
        ones_beside(values)
        put(own[pl.ds(0, PIECE), :], keys, values, pl.ds(0, PIECE))
        queries_square = largest_square(rows_out[...])
        plain = queries_square * largest_square(keys[...]) <= SAFE
        peak_out[pl.ds(FLAG, 8), :] = jnp.full((8, HD), jnp.where(plain, queries_square, UNSAFE))

        @pl.when(plain)
        def _():
            peak_out[pl.ds(0, FLAG), :] = jnp.zeros((FLAG, HD), jnp.float32)

            def tile(index, carry):
                rows = pl.ds(pl.multiple_of(index * TILE, TILE), TILE)
                summed_out[rows, :] = plain_step(None, rows_out[rows, :], keys[...], values[...])
                return carry

            lax.fori_loop(0, FLAG // TILE, tile, 0)

        @pl.when(jnp.logical_not(plain))
        def _():
            def tile(index, carry):
                rows = pl.ds(pl.multiple_of(index * TOK, TOK), TOK)
                peak, summed = softmax_step(None, None, rows_out[rows, :], keys[...], values[...])
                peak_out[rows, :] = jnp.broadcast_to(peak, (TOK, HD))
                summed_out[rows, :] = summed
                return carry

            lax.fori_loop(0, HEADS, tile, 0)


def still_plain(peak, keys):
    return jnp.max(peak[pl.ds(FLAG, 8), :]) * largest_square(keys[...]) <= SAFE


def middle_kernel(
    table, queries, b1, b2, peak_in, summed_in, peak_out, summed_out, keys, values
):
    here = Place(table)

    @pl.when(here.has_long(here.position))
    def _():
        ones_beside(values)
        for index, message in enumerate((b1, b2)):
            put(message[pl.ds(0, PIECE), :], keys, values, pl.ds(index * PIECE, PIECE))
        plain = still_plain(peak_in, keys)

        @pl.when(plain)
        def _():
            def tile(index, carry):
                rows = pl.ds(pl.multiple_of(index * TILE, TILE), TILE)
                query, summed = queries[rows, :], summed_in[rows, :]
                for part in (pl.ds(0, PIECE), pl.ds(PIECE, PIECE)):
                    summed = plain_step(summed, query, keys[part, :], values[part, :])
                summed_out[rows, :] = summed
                return carry

            lax.fori_loop(0, FLAG // TILE, tile, 0)

        @pl.when(jnp.logical_not(plain))
        def _():
            def tile(index, carry):
                rows = pl.ds(pl.multiple_of(index * TOK, TOK), TOK)
                peak, summed = softmax_step(
                    peak_in[rows, :1], summed_in[rows, :], queries[rows, :], keys[...], values[...])
                peak_out[rows, :] = jnp.broadcast_to(peak, (TOK, HD))
                summed_out[rows, :] = summed
                return carry

            lax.fori_loop(0, HEADS, tile, 0)
            peak_out[pl.ds(FLAG, 8), :] = jnp.full((8, HD), UNSAFE, jnp.float32)


def last_kernel(low, high, table, rows_in, own, b1, b2, b3, small, peak_in, summed_in, *refs):
    here = Place(table)
    count = high - low
    if low == 0:
        queries, n0, n1, n2, n3, out, rest, keys, values, result, held, *small_scratch = refs
        pure = jnp.logical_not(here.has_long(here.position))

        @pl.when(jnp.logical_not(pure))
        def _():
            held[...] = small[...]

        small_kernel(
            False, table, queries, n0, n1, n2, n3, b1, b2, b3, held, *small_scratch)
        small = held
        rest[...] = held[:, pl.ds(high * HD, (HEADS - high) * HD)]
    else:
        out, keys, values, result = refs[-4:]

    @pl.when(here.has_long(here.position))
    def _():
        ones_beside(values)
        put(b3[pl.ds(0, PIECE), :], keys, values, pl.ds(0, PIECE))
        for extra in range(EXTRA):
            grain = here.start + extra
            rows = pl.ds(PIECE + extra * GRAIN, GRAIN)
            group = jnp.where(here.core == 0, grain // 16, grain // 4 % 4)
            for message, by in zip((own, b1, b2, b3), OFFSETS):
                @pl.when(group == (here.outer + by + 4) % 4)
                def _():
                    put(message[rows, :], keys, values, rows)

        plain = still_plain(peak_in, keys)

        @pl.when(plain)
        def _():
            rows = pl.ds(low * TOK, count * TOK)
            summed = plain_step(summed_in[rows, :], rows_in[rows, :], keys[...], values[...])
            result[...] = (summed[:, :HD] / summed[:, HD:]).astype(jnp.bfloat16)

        @pl.when(jnp.logical_not(plain))
        def _():
            def tile(index, carry):
                rows = pl.ds(pl.multiple_of((low + index) * TOK, TOK), TOK)
                _, summed = softmax_step(
                    peak_in[rows, :1], summed_in[rows, :], rows_in[rows, :], keys[...], values[...])
                result[pl.ds(pl.multiple_of(index * TOK, TOK), TOK), :] = (
                    summed[:, :HD] / summed[:, HD:]).astype(jnp.bfloat16)
                return carry

            lax.fori_loop(0, count, tile, 0)

        for index in range(count):
            out[:, pl.ds(index * HD, HD)] = result[pl.ds(index * TOK, TOK), :]

    for grain in range(GRAINS):
        at = here.position * GRAINS + grain
        tokens = pl.ds(grain * GRAIN, GRAIN)

        @pl.when(jnp.where(here.zh == 0, at < here.start, at >= here.stop))
        def _():
            columns = pl.ds(0, count * HD)
            out[tokens, :] = small[tokens, columns]


def small_kernel(straddle, table, *refs):
    if straddle:
        far, queries, n0, r1, r2, r3, r4, _, out = refs[:9]
    else:
        queries, n0, n1, n2, n3, b1, b2, b3, out = refs[:9]
    keys, values, result = refs[-3:]
    here, lengths = Place(table), Lengths(table)
    long_here, small_here = here.has_long(here.position), here.has_small(here.position)

    @pl.when(small_here & (long_here if straddle else jnp.logical_not(long_here)))
    def _():
        def block(source, row, position):
            put(source[pl.ds(row, TOK), :], keys, values, rows_of(position * TOK, TOK))

        ones_beside(values)
        if straddle:
            values[:, :HD] = jnp.zeros((PLANE_TOK + SMALL, HD), jnp.bfloat16)
            block(n0, 0, here.position)
            away = jnp.where(here.zh == 0, -1, 1)
            for step in range(1, 1 + NEAR_BLOCKS + FAR_BLOCKS):
                position = here.position + away * step
                inside = (position >= 0) & (position < 16)
                source, row = ((r1, r2, r3)[step - 1], 0) if step <= NEAR_BLOCKS else (
                    r4, (step - 1 - NEAR_BLOCKS) * TOK)
                if step > NEAR_BLOCKS:
                    inside = inside & (far[0] == 1)

                @pl.when(inside)
                def _():
                    block(source, row, position)
        else:
            values[pl.ds(PLANE_TOK, SMALL), :HD] = jnp.zeros((SMALL, HD), jnp.bfloat16)
            for inner, near in enumerate(OFFSETS):
                block((n0, n1, n2, n3)[inner], 0, here.at(0, near))
                for message, by in zip((b1, b2, b3), OFFSETS[1:]):
                    block(message, inner * TOK, here.at(by, near))

        column = lax.broadcasted_iota(jnp.int32, (1, SMALL), 1)

        def one_grain(grain, carry):
            first, end = bounds(lengths, (here.zh * 16 + here.position) * GRAINS + grain)

            @pl.when(end - first != LONG_GRAINS)
            def _():
                tokens = rows_of(grain * GRAIN, GRAIN)
                query = stacked(queries, range(HEADS), tokens.start, GRAIN)
                offset = (first - here.zh * PLANE_GRAINS) * GRAIN
                width = (end - first) * GRAIN

                def step(index, state):
                    part = rows_of(offset + index * SMALL, SMALL)
                    return softmax_step(
                        *state, query, keys[part, :], values[part, :],
                        column < width - index * SMALL)

                initial = (
                    jnp.full((HEADS * GRAIN, 1), LOWEST, jnp.float32),
                    jnp.zeros((HEADS * GRAIN, 2 * HD), jnp.float32),
                )
                _, summed = lax.fori_loop(0, (width + SMALL - 1) // SMALL, step, initial)
                result[...] = (summed[:, :HD] / summed[:, HD:]).astype(jnp.bfloat16)
                for head in range(HEADS):
                    out[tokens, pl.ds(head * HD, HD)] = result[pl.ds(head * GRAIN, GRAIN), :]

            return carry

        lax.fori_loop(0, GRAINS, one_grain, 0)


def scratch(rows):
    return [pltpu.VMEM((rows, HD), jnp.bfloat16), pltpu.VMEM((rows, 2 * HD), jnp.bfloat16)]


def cost(keys, heads=HEADS):
    rows = heads * TOK
    return pl.CostEstimate(
        flops=6 * rows * keys * HD, bytes_accessed=rows * HD * 4, transcendentals=rows * keys)


STATE = [
    jax.ShapeDtypeStruct((FLAG + 8, HD), jnp.float32),
    jax.ShapeDtypeStruct((HEADS * TOK, 2 * HD), jnp.float32),
]
PARAMS = pltpu.CompilerParams(vmem_limit_bytes=28 * 2**20)


def attend_own(table, queries, own):
    rows = jax.ShapeDtypeStruct((HEADS * TOK, HD), jnp.bfloat16)
    return pl.pallas_call(
        own_kernel,
        out_shape=[rows] + STATE,
        in_specs=[SMEM, VMEM, VMEM],
        out_specs=[VMEM] * 3,
        scratch_shapes=scratch(PIECE),
        compiler_params=PARAMS,
        cost_estimate=cost(PIECE),
        name="own",
    )(table, queries, own)


def attend_middle(table, rows, messages, state, after):
    def kernel(*refs):
        middle_kernel(*refs[:6], *refs[7:])

    return pl.pallas_call(
        kernel,
        out_shape=STATE,
        in_specs=[SMEM] + [VMEM] * 5 + [HBM],
        out_specs=[VMEM] * 2,
        scratch_shapes=scratch(2 * PIECE),
        input_output_aliases={4: 0, 5: 1},
        compiler_params=PARAMS,
        cost_estimate=cost(2 * PIECE),
        name="middle",
    )(table, rows, *messages, *state, after)


def attend_last(low, high, table, blocks, more):
    shapes = [jax.ShapeDtypeStruct((TOK, (high - low) * HD), jnp.bfloat16)]
    scratches = scratch(MESSAGE) + [pltpu.VMEM(((high - low) * TOK, HD), jnp.bfloat16)]
    if low == 0:
        shapes.append(jax.ShapeDtypeStruct((TOK, (HEADS - high) * HD), jnp.bfloat16))
        scratches += [pltpu.VMEM((TOK, HEADS * HD), jnp.bfloat16)] + scratch(PLANE_TOK + SMALL) + [
            pltpu.VMEM((HEADS * GRAIN, HD), jnp.bfloat16)]
    return pl.pallas_call(
        functools.partial(last_kernel, low, high),
        out_shape=shapes,
        in_specs=[SMEM] + [VMEM] * (len(blocks) + len(more)),
        out_specs=[VMEM] * len(shapes),
        scratch_shapes=scratches,
        compiler_params=PARAMS,
        cost_estimate=cost(MESSAGE, high - low),
        name="last",
    )(table, *blocks, *more)


def attend_small(scalars, blocks):
    return pl.pallas_call(
        functools.partial(small_kernel, True),
        out_shape=jax.ShapeDtypeStruct((TOK, HEADS * HD), jnp.bfloat16),
        in_specs=[SMEM] * len(scalars) + [VMEM] * len(blocks),
        out_specs=VMEM,
        scratch_shapes=scratch(PLANE_TOK + SMALL) + [pltpu.VMEM((HEADS * GRAIN, HD), jnp.bfloat16)],
        compiler_params=PARAMS,
        cost_estimate=cost(TOK),
        name="small",
    )(*scalars, *blocks)


def add_products(total, groups, weight, parts):
    for index, head, part in parts:
        rows = pl.ds(pl.multiple_of(groups[index] * HEADS * HD + head * HD, HD), part.shape[1])
        term = jnp.dot(part[...], weight[rows, :], preferred_element_type=jnp.float32)
        total = term if total is None else total + term
    return total


def near_kernel(where, groups, weight, *refs):
    parts, (out, held, sem) = refs[:len(where)], refs[len(where):]
    copy = pltpu.make_async_copy(weight, held, sem)
    copy.start()
    copy.wait()
    out[...] = add_products(None, groups, held, [(*w, p) for w, p in zip(where, parts)])


def rest_kernel(where, groups, weight, *refs):
    parts, (before, out) = refs[:len(where)], refs[len(where):]
    total = add_products(before[...], groups, weight, [(*w, p) for w, p in zip(where, parts)])
    out[...] = total.astype(out.dtype)


def project(where, groups, weight, parts, before=None):
    depth = sum(part.shape[1] for part in parts)
    shape = (TOK, weight.shape[1])
    if before is None:
        kernel, operands, place, scratches = near_kernel, parts, HBM, [pltpu.SemaphoreType.DMA]
        out_shape = [
            jax.ShapeDtypeStruct(shape, jnp.float32), jax.ShapeDtypeStruct(weight.shape, weight.dtype)]
    else:
        kernel, operands, place, scratches = rest_kernel, [*parts, before], VMEM, []
        out_shape = [jax.ShapeDtypeStruct(shape, jnp.bfloat16)]
    return pl.pallas_call(
        functools.partial(kernel, where),
        out_shape=out_shape,
        in_specs=[SMEM, place] + [VMEM] * len(operands),
        out_specs=[VMEM] * len(out_shape),
        scratch_shapes=scratches,
        compiler_params=pltpu.CompilerParams(vmem_limit_bytes=12 * 2**20),
        cost_estimate=pl.CostEstimate(
            flops=2 * TOK * depth * weight.shape[1], bytes_accessed=2 * depth * weight.shape[1],
            transcendentals=0),
        name="project",
    )(groups, weight, *operands)


def per_device(queries, keys, values, doc_lengths, out_weight):
    zh, y, x, zl, c = (lax.axis_index(a) for a in ("zh", "y", "x", "zl", "c"))
    table = jnp.concatenate([jnp.stack([zh, y, x, c]).astype(jnp.int32), doc_lengths])
    native = join(keys, values)
    other = swap(native, "zh")
    natives = [native] + [move(native, 0, -k) for k in OFFSETS[1:]]
    others = [other] + [move(other, 0, -k) for k in OFFSETS[1:]]
    rings = [ring(native, step) for step in range(1, 1 + NEAR_BLOCKS)]
    own, *sent, is_far = pack(table, natives, others, rings)
    messages = [move(block, -k, 0) for block, k in zip(sent, OFFSETS[1:])]
    nothing = jnp.zeros((FAR_BLOCKS * TOK, 2 * HD), jnp.bfloat16)

    def fetch(block):
        def step(index, carry):
            block, blocks = carry
            block = ring(block, 1)
            at = jnp.maximum(index - NEAR_BLOCKS, 0) * TOK
            return block, lax.dynamic_update_slice_in_dim(blocks, block, at, 0)

        return lax.fori_loop(0, NEAR_BLOCKS + FAR_BLOCKS, step, (block, nothing))[1]

    beyond_rings = lax.cond(is_far[0] == 1, fetch, lambda block: nothing, native)
    rows, *state = attend_own(table, queries, own)
    small = attend_small((table, is_far), (queries, native, *rings, beyond_rings, rows))
    state = attend_middle(table, rows, messages[:2], state, small)
    (first, middle), (second, _) = CHUNKS
    some, rest = attend_last(
        first, middle, table, (rows, own, *messages, small, *state), (queries, *natives))
    chunks = [some] + list(attend_last(
        second, HEADS, table, (rows, own, *messages, rest, *state), ()))
    across = [swap(part, "zl") for part in chunks]
    beside = [swap(part, "c") for part in chunks]
    group = (zl * 2 + c).astype(jnp.int32)
    groups = jnp.stack([group, group ^ 1, group ^ 2, group ^ 3])
    mixed, weight = project(
        [(0, first), (0, second), (1, first), (1, second)], groups, out_weight, chunks + beside)
    across, mixed = lax.optimization_barrier((across, mixed))
    beyond = [swap(part, "c") for part in across]
    return project(
        [(2, first), (3, first), (2, second), (3, second)], groups, weight,
        [across[0], beyond[0], across[1], beyond[1]], mixed)[0]


def solution(mesh):
    fine = Mesh(np.asarray(mesh.devices).reshape(2, 4, 4, 2, 2), ("zh", "y", "x", "zl", "c"))
    seq, kv = ("zh", "y", "x"), ("zl", "c")
    return jax.shard_map(
        per_device,
        mesh=fine,
        in_specs=(P(seq, kv), P(seq, kv), P(seq, kv), P(), P(None, kv)),
        out_specs=P(seq, kv),
        check_vma=False,
    )
```

```python
import functools

import jax
import jax.numpy as jnp
import numpy as np
from jax import lax
from jax.experimental import pallas as pl
from jax.experimental.pallas import tpu as pltpu
from jax.sharding import Mesh, PartitionSpec as P

HD = 128
GRAIN = 64
TOK = 256
HEADS = 7
GRAINS = TOK // GRAIN
DOCS = 16
LONG_GRAINS = 68
PLANE_GRAINS = 64
PLANE_TOK = PLANE_GRAINS * GRAIN
EXTRA = LONG_GRAINS - PLANE_GRAINS
PIECE = 4 * TOK
MESSAGE = PIECE + EXTRA * GRAIN
SMALL = 256
NEAR_BLOCKS = 3
FAR_BLOCKS = 9
CHUNKS = ((0, 5), (5, 7))
TILE = 896
FLAG = HEADS * TOK
SCALE = 1.4426950408889634 / HD**0.5
LOWEST = -1e30
SAFE = (90.0 / SCALE) ** 2
UNSAFE = 1e30
OFFSETS = (0, -1, 1, 2)

SMEM = pl.BlockSpec(memory_space=pltpu.SMEM)
VMEM = pl.BlockSpec(memory_space=pltpu.VMEM)
HBM = pl.BlockSpec(memory_space=pltpu.HBM)


def turn(by_first, by_second):
    pairs = []
    for y in range(4):
        for x in range(4):
            pairs.append((y, x, 0, (y + by_first) % 4, (x + by_second) % 4))
            pairs.append((y, x, 1, (y + by_second) % 4, (x + by_first) % 4))
    return [((y * 4 + x) * 2 + c, (to_y * 4 + to_x) * 2 + c) for y, x, c, to_y, to_x in pairs]


def move(block, by_first, by_second):
    return lax.ppermute(block, ("y", "x", "c"), turn(by_first, by_second))


def ring(block, step):
    pairs = []
    for at in range(16):
        pairs.append((at, (at + step) % 16))
        pairs.append((16 + at, 16 + (at - step) % 16))
    return lax.ppermute(block, ("zh", "y", "x"), pairs)


def swap(block, axis):
    return lax.ppermute(block, axis, [(0, 1), (1, 0)])


class Lengths:
    def __init__(self, table):
        self.table = table

    def __getitem__(self, doc):
        return self.table[4 + doc]


class Place:
    def __init__(self, table):
        lengths = Lengths(table)
        self.zh, y, x, self.core = table[0], table[1], table[2], table[3]
        self.inner = jnp.where(self.core == 0, x, y)
        self.outer = jnp.where(self.core == 0, y, x)
        self.position = y * 4 + x
        total, start = jnp.int32(0), jnp.int32(0)
        for doc in range(DOCS):
            start = jnp.where(lengths[doc] == LONG_GRAINS, total, start)
            total = total + lengths[doc]
        self.start, self.stop = start, start + EXTRA

    def at(self, outer_by, inner_by):
        outer, inner = (self.outer + outer_by + 4) % 4, (self.inner + inner_by + 4) % 4
        return jnp.where(self.core == 0, outer * 4 + inner, inner * 4 + outer)

    def has_long(self, position):
        return jnp.where(self.zh == 0, position * 4 + 3 >= self.start, position * 4 < self.stop)

    def has_small(self, position):
        return jnp.where(self.zh == 0, position * 4 < self.start, position * 4 + 3 >= self.stop)


def rows_of(start, count):
    return pl.ds(pl.multiple_of(start, GRAIN), count)


def bounds(lengths, grain):
    first, end, total = jnp.int32(0), jnp.int32(0), jnp.int32(0)
    for doc in range(DOCS):
        after = total + lengths[doc]
        inside = (total <= grain) & (grain < after)
        first = jnp.where(inside, total, first)
        end = jnp.where(inside, after, end)
        total = after
    return first, end


def join_kernel(keys, values, out, sems):
    copies = [
        pltpu.make_async_copy(keys, out.at[:, pl.ds(0, HD)], sems.at[0]),
        pltpu.make_async_copy(values, out.at[:, pl.ds(HD, HD)], sems.at[1]),
    ]
    for copy in copies:
        copy.start()
    for copy in copies:
        copy.wait()


def join(keys, values):
    return pl.pallas_call(
        join_kernel,
        out_shape=jax.ShapeDtypeStruct((TOK, 2 * HD), jnp.bfloat16),
        in_specs=[HBM, HBM],
        out_specs=VMEM,
        scratch_shapes=[pltpu.SemaphoreType.DMA((2,))],
        name="join",
    )(keys, values)


def pack_kernel(table, *refs):
    natives, others, (own, m1, m2, m3, far) = refs[:4], refs[4:8], refs[-5:]
    here = Place(table)
    for inner in range(4):
        cut = jnp.clip(here.start - here.at(0, OFFSETS[inner]) * 4, 0, 4)
        for plane, blocks in ((here.zh, natives), (1 - here.zh, others)):
            @pl.when(cut == 4 * plane)
            def _():
                own[pl.ds(inner * TOK, TOK), :] = blocks[inner][...]

            @pl.when((cut > 0) & (cut < 4))
            def _():
                for grain in range(GRAINS):
                    @pl.when((grain < cut).astype(jnp.int32) == plane)
                    def _():
                        own[pl.ds(inner * TOK + grain * GRAIN, GRAIN), :] = blocks[inner][
                            pl.ds(grain * GRAIN, GRAIN), :]

    for extra in range(EXTRA):
        grain = here.start + extra
        for inner in range(4):
            for plane, blocks in ((1, natives), (0, others)):
                @pl.when((grain // 4 == here.at(0, OFFSETS[inner])) & (here.zh == plane))
                def _():
                    own[pl.ds(PIECE + extra * GRAIN, GRAIN), :] = blocks[inner][
                        rows_of(grain % 4 * GRAIN, GRAIN), :]

    for index, out in enumerate((m1, m2, m3)):
        to_long = here.has_long(here.at(-OFFSETS[index + 1], 0))

        @pl.when(to_long)
        def _():
            out[...] = own[...]

        @pl.when(jnp.logical_not(to_long))
        def _():
            for inner in range(4):
                out[pl.ds(inner * TOK, TOK), :] = natives[inner][...]

    lengths = Lengths(table)
    start, end = here.start, here.start + LONG_GRAINS
    before, after = start - start % 4, end + (4 - end % 4) % 4
    reach_before = jnp.where(start % 4 == 0, 0, before - bounds(lengths, before)[0])
    reach_after = jnp.where(end % 4 == 0, 0, bounds(lengths, after - 1)[1] - after)
    far[0] = (jnp.maximum(reach_before, reach_after) > NEAR_BLOCKS * 4).astype(jnp.int32)


def pack(table, natives, others, after):
    return pl.pallas_call(
        pack_kernel,
        out_shape=[jax.ShapeDtypeStruct((MESSAGE, 2 * HD), jnp.bfloat16)] * 4 + [
            jax.ShapeDtypeStruct((1,), jnp.int32)],
        in_specs=[SMEM] + [VMEM] * 8 + [HBM] * len(after),
        out_specs=[VMEM] * 4 + [SMEM],
        compiler_params=PARAMS,
        name="pack",
    )(table, *natives, *others, *after)


def put(block, keys, values, rows):
    keys[rows, :] = block[:, :HD]
    values[rows, :HD] = block[:, HD:]


def ones_beside(values):
    values[:, HD:] = jnp.ones((values.shape[0], HD), jnp.bfloat16)


def largest_square(block):
    block = block.astype(jnp.float32)
    return jnp.max(jnp.sum(block * block, axis=1, keepdims=True))


def plain_step(summed, query, keys, values):
    scores = lax.dot_general(
        query, keys, (((1,), (1,)), ((), ())), preferred_element_type=jnp.float32
    )
    weights = jnp.exp2(scores * SCALE).astype(jnp.bfloat16)
    product = jnp.dot(weights, values, preferred_element_type=jnp.float32)
    return product if summed is None else summed + product


def softmax_step(peak, summed, query, keys, values, allowed=None):
    scores = lax.dot_general(
        query, keys, (((1,), (1,)), ((), ())), preferred_element_type=jnp.float32
    )
    scores = scores * SCALE
    if allowed is not None:
        scores = jnp.where(allowed, scores, LOWEST)
    top = jnp.max(scores, axis=1, keepdims=True)
    peak_new = top if peak is None else jnp.maximum(peak, top)
    weights = jnp.exp2(scores - peak_new).astype(jnp.bfloat16)
    product = jnp.dot(weights, values, preferred_element_type=jnp.float32)
    if peak is not None:
        product = summed * jnp.exp2(peak - peak_new) + product
    return peak_new, product


def stacked(queries, heads, start, count):
    return jnp.concatenate(
        [queries[pl.ds(start, count), pl.ds(head * HD, HD)] for head in heads], axis=0
    )


def own_kernel(table, queries, own, rows_out, peak_out, summed_out, keys, values):
    here = Place(table)

    @pl.when(here.has_long(here.position))
    def _():
        for head in range(HEADS):
            rows_out[pl.ds(head * TOK, TOK), :] = queries[:, pl.ds(head * HD, HD)]
        ones_beside(values)
        put(own[pl.ds(0, PIECE), :], keys, values, pl.ds(0, PIECE))
        queries_square = largest_square(rows_out[...])
        plain = queries_square * largest_square(keys[...]) <= SAFE
        peak_out[pl.ds(FLAG, 8), :] = jnp.full((8, HD), jnp.where(plain, queries_square, UNSAFE))

        @pl.when(plain)
        def _():
            peak_out[pl.ds(0, FLAG), :] = jnp.zeros((FLAG, HD), jnp.float32)

            def tile(index, carry):
                rows = pl.ds(pl.multiple_of(index * TILE, TILE), TILE)
                summed_out[rows, :] = plain_step(None, rows_out[rows, :], keys[...], values[...])
                return carry

            lax.fori_loop(0, FLAG // TILE, tile, 0)

        @pl.when(jnp.logical_not(plain))
        def _():
            def tile(index, carry):
                rows = pl.ds(pl.multiple_of(index * TOK, TOK), TOK)
                peak, summed = softmax_step(None, None, rows_out[rows, :], keys[...], values[...])
                peak_out[rows, :] = jnp.broadcast_to(peak, (TOK, HD))
                summed_out[rows, :] = summed
                return carry

            lax.fori_loop(0, HEADS, tile, 0)


def still_plain(peak, keys):
    return jnp.max(peak[pl.ds(FLAG, 8), :]) * largest_square(keys[...]) <= SAFE


def middle_kernel(
    table, queries, b1, b2, peak_in, summed_in, peak_out, summed_out, keys, values
):
    here = Place(table)

    @pl.when(here.has_long(here.position))
    def _():
        ones_beside(values)
        for index, message in enumerate((b1, b2)):
            put(message[pl.ds(0, PIECE), :], keys, values, pl.ds(index * PIECE, PIECE))
        plain = still_plain(peak_in, keys)

        @pl.when(plain)
        def _():
            def tile(index, carry):
                rows = pl.ds(pl.multiple_of(index * TILE, TILE), TILE)
                query, summed = queries[rows, :], summed_in[rows, :]
                for part in (pl.ds(0, PIECE), pl.ds(PIECE, PIECE)):
                    summed = plain_step(summed, query, keys[part, :], values[part, :])
                summed_out[rows, :] = summed
                return carry

            lax.fori_loop(0, FLAG // TILE, tile, 0)

        @pl.when(jnp.logical_not(plain))
        def _():
            def tile(index, carry):
                rows = pl.ds(pl.multiple_of(index * TOK, TOK), TOK)
                peak, summed = softmax_step(
                    peak_in[rows, :1], summed_in[rows, :], queries[rows, :], keys[...], values[...])
                peak_out[rows, :] = jnp.broadcast_to(peak, (TOK, HD))
                summed_out[rows, :] = summed
                return carry

            lax.fori_loop(0, HEADS, tile, 0)
            peak_out[pl.ds(FLAG, 8), :] = jnp.full((8, HD), UNSAFE, jnp.float32)


def last_kernel(low, high, table, rows_in, own, b1, b2, b3, small, peak_in, summed_in, *refs):
    here = Place(table)
    count = high - low
    if low == 0:
        queries, n0, n1, n2, n3, out, rest, keys, values, result, held, *small_scratch = refs
        pure = jnp.logical_not(here.has_long(here.position))

        @pl.when(jnp.logical_not(pure))
        def _():
            held[...] = small[...]

        small_kernel(
            False, table, queries, n0, n1, n2, n3, b1, b2, b3, held, *small_scratch)
        small = held
        rest[...] = held[:, pl.ds(high * HD, (HEADS - high) * HD)]
    else:
        out, keys, values, result = refs[-4:]

    @pl.when(here.has_long(here.position))
    def _():
        ones_beside(values)
        put(b3[pl.ds(0, PIECE), :], keys, values, pl.ds(0, PIECE))
        for extra in range(EXTRA):
            grain = here.start + extra
            rows = pl.ds(PIECE + extra * GRAIN, GRAIN)
            group = jnp.where(here.core == 0, grain // 16, grain // 4 % 4)
            for message, by in zip((own, b1, b2, b3), OFFSETS):
                @pl.when(group == (here.outer + by + 4) % 4)
                def _():
                    put(message[rows, :], keys, values, rows)

        plain = still_plain(peak_in, keys)

        @pl.when(plain)
        def _():
            rows = pl.ds(low * TOK, count * TOK)
            summed = plain_step(summed_in[rows, :], rows_in[rows, :], keys[...], values[...])
            result[...] = (summed[:, :HD] / summed[:, HD:]).astype(jnp.bfloat16)

        @pl.when(jnp.logical_not(plain))
        def _():
            def tile(index, carry):
                rows = pl.ds(pl.multiple_of((low + index) * TOK, TOK), TOK)
                _, summed = softmax_step(
                    peak_in[rows, :1], summed_in[rows, :], rows_in[rows, :], keys[...], values[...])
                result[pl.ds(pl.multiple_of(index * TOK, TOK), TOK), :] = (
                    summed[:, :HD] / summed[:, HD:]).astype(jnp.bfloat16)
                return carry

            lax.fori_loop(0, count, tile, 0)

        for index in range(count):
            out[:, pl.ds(index * HD, HD)] = result[pl.ds(index * TOK, TOK), :]

    for grain in range(GRAINS):
        at = here.position * GRAINS + grain
        tokens = pl.ds(grain * GRAIN, GRAIN)

        @pl.when(jnp.where(here.zh == 0, at < here.start, at >= here.stop))
        def _():
            columns = pl.ds(0, count * HD)
            out[tokens, :] = small[tokens, columns]


def small_kernel(straddle, table, *refs):
    if straddle:
        far, queries, n0, r1, r2, r3, r4, _, out = refs[:9]
    else:
        queries, n0, n1, n2, n3, b1, b2, b3, out = refs[:9]
    keys, values, result = refs[-3:]
    here, lengths = Place(table), Lengths(table)
    long_here, small_here = here.has_long(here.position), here.has_small(here.position)

    @pl.when(small_here & (long_here if straddle else jnp.logical_not(long_here)))
    def _():
        def block(source, row, position):
            put(source[pl.ds(row, TOK), :], keys, values, rows_of(position * TOK, TOK))

        ones_beside(values)
        if straddle:
            values[:, :HD] = jnp.zeros((PLANE_TOK + SMALL, HD), jnp.bfloat16)
            block(n0, 0, here.position)
            away = jnp.where(here.zh == 0, -1, 1)
            for step in range(1, 1 + NEAR_BLOCKS + FAR_BLOCKS):
                position = here.position + away * step
                inside = (position >= 0) & (position < 16)
                source, row = ((r1, r2, r3)[step - 1], 0) if step <= NEAR_BLOCKS else (
                    r4, (step - 1 - NEAR_BLOCKS) * TOK)
                if step > NEAR_BLOCKS:
                    inside = inside & (far[0] == 1)

                @pl.when(inside)
                def _():
                    block(source, row, position)
        else:
            values[pl.ds(PLANE_TOK, SMALL), :HD] = jnp.zeros((SMALL, HD), jnp.bfloat16)
            for inner, near in enumerate(OFFSETS):
                block((n0, n1, n2, n3)[inner], 0, here.at(0, near))
                for message, by in zip((b1, b2, b3), OFFSETS[1:]):
                    block(message, inner * TOK, here.at(by, near))

        column = lax.broadcasted_iota(jnp.int32, (1, SMALL), 1)

        def one_grain(grain, carry):
            first, end = bounds(lengths, (here.zh * 16 + here.position) * GRAINS + grain)

            @pl.when(end - first != LONG_GRAINS)
            def _():
                tokens = rows_of(grain * GRAIN, GRAIN)
                query = stacked(queries, range(HEADS), tokens.start, GRAIN)
                offset = (first - here.zh * PLANE_GRAINS) * GRAIN
                width = (end - first) * GRAIN

                def step(index, state):
                    part = rows_of(offset + index * SMALL, SMALL)
                    return softmax_step(
                        *state, query, keys[part, :], values[part, :],
                        column < width - index * SMALL)

                initial = (
                    jnp.full((HEADS * GRAIN, 1), LOWEST, jnp.float32),
                    jnp.zeros((HEADS * GRAIN, 2 * HD), jnp.float32),
                )
                _, summed = lax.fori_loop(0, (width + SMALL - 1) // SMALL, step, initial)
                result[...] = (summed[:, :HD] / summed[:, HD:]).astype(jnp.bfloat16)
                for head in range(HEADS):
                    out[tokens, pl.ds(head * HD, HD)] = result[pl.ds(head * GRAIN, GRAIN), :]

            return carry

        lax.fori_loop(0, GRAINS, one_grain, 0)


def scratch(rows):
    return [pltpu.VMEM((rows, HD), jnp.bfloat16), pltpu.VMEM((rows, 2 * HD), jnp.bfloat16)]


def cost(keys, heads=HEADS):
    rows = heads * TOK
    return pl.CostEstimate(
        flops=6 * rows * keys * HD, bytes_accessed=rows * HD * 4, transcendentals=rows * keys)


STATE = [
    jax.ShapeDtypeStruct((FLAG + 8, HD), jnp.float32),
    jax.ShapeDtypeStruct((HEADS * TOK, 2 * HD), jnp.float32),
]
PARAMS = pltpu.CompilerParams(vmem_limit_bytes=28 * 2**20)


def attend_own(table, queries, own):
    rows = jax.ShapeDtypeStruct((HEADS * TOK, HD), jnp.bfloat16)
    return pl.pallas_call(
        own_kernel,
        out_shape=[rows] + STATE,
        in_specs=[SMEM, VMEM, VMEM],
        out_specs=[VMEM] * 3,
        scratch_shapes=scratch(PIECE),
        compiler_params=PARAMS,
        cost_estimate=cost(PIECE),
        name="own",
    )(table, queries, own)


def attend_middle(table, rows, messages, state, after):
    def kernel(*refs):
        middle_kernel(*refs[:6], *refs[7:])

    return pl.pallas_call(
        kernel,
        out_shape=STATE,
        in_specs=[SMEM] + [VMEM] * 5 + [HBM],
        out_specs=[VMEM] * 2,
        scratch_shapes=scratch(2 * PIECE),
        input_output_aliases={4: 0, 5: 1},
        compiler_params=PARAMS,
        cost_estimate=cost(2 * PIECE),
        name="middle",
    )(table, rows, *messages, *state, after)


def attend_last(low, high, table, blocks, more):
    shapes = [jax.ShapeDtypeStruct((TOK, (high - low) * HD), jnp.bfloat16)]
    scratches = scratch(MESSAGE) + [pltpu.VMEM(((high - low) * TOK, HD), jnp.bfloat16)]
    if low == 0:
        shapes.append(jax.ShapeDtypeStruct((TOK, (HEADS - high) * HD), jnp.bfloat16))
        scratches += [pltpu.VMEM((TOK, HEADS * HD), jnp.bfloat16)] + scratch(PLANE_TOK + SMALL) + [
            pltpu.VMEM((HEADS * GRAIN, HD), jnp.bfloat16)]
    return pl.pallas_call(
        functools.partial(last_kernel, low, high),
        out_shape=shapes,
        in_specs=[SMEM] + [VMEM] * (len(blocks) + len(more)),
        out_specs=[VMEM] * len(shapes),
        scratch_shapes=scratches,
        compiler_params=PARAMS,
        cost_estimate=cost(MESSAGE, high - low),
        name="last",
    )(table, *blocks, *more)


def attend_small(scalars, blocks):
    return pl.pallas_call(
        functools.partial(small_kernel, True),
        out_shape=jax.ShapeDtypeStruct((TOK, HEADS * HD), jnp.bfloat16),
        in_specs=[SMEM] * len(scalars) + [VMEM] * len(blocks),
        out_specs=VMEM,
        scratch_shapes=scratch(PLANE_TOK + SMALL) + [pltpu.VMEM((HEADS * GRAIN, HD), jnp.bfloat16)],
        compiler_params=PARAMS,
        cost_estimate=cost(TOK),
        name="small",
    )(*scalars, *blocks)


def add_products(total, groups, weight, parts):
    for index, head, part in parts:
        rows = pl.ds(pl.multiple_of(groups[index] * HEADS * HD + head * HD, HD), part.shape[1])
        term = jnp.dot(part[...], weight[rows, :], preferred_element_type=jnp.float32)
        total = term if total is None else total + term
    return total


def near_kernel(where, groups, weight, *refs):
    parts, (out, held, sem) = refs[:len(where)], refs[len(where):]
    copy = pltpu.make_async_copy(weight, held, sem)
    copy.start()
    copy.wait()
    out[...] = add_products(None, groups, held, [(*w, p) for w, p in zip(where, parts)])


def rest_kernel(where, groups, weight, *refs):
    parts, (before, out) = refs[:len(where)], refs[len(where):]
    total = add_products(before[...], groups, weight, [(*w, p) for w, p in zip(where, parts)])
    out[...] = total.astype(out.dtype)


def project(where, groups, weight, parts, before=None):
    depth = sum(part.shape[1] for part in parts)
    shape = (TOK, weight.shape[1])
    if before is None:
        kernel, operands, place, scratches = near_kernel, parts, HBM, [pltpu.SemaphoreType.DMA]
        out_shape = [
            jax.ShapeDtypeStruct(shape, jnp.float32), jax.ShapeDtypeStruct(weight.shape, weight.dtype)]
    else:
        kernel, operands, place, scratches = rest_kernel, [*parts, before], VMEM, []
        out_shape = [jax.ShapeDtypeStruct(shape, jnp.bfloat16)]
    return pl.pallas_call(
        functools.partial(kernel, where),
        out_shape=out_shape,
        in_specs=[SMEM, place] + [VMEM] * len(operands),
        out_specs=[VMEM] * len(out_shape),
        scratch_shapes=scratches,
        compiler_params=pltpu.CompilerParams(vmem_limit_bytes=12 * 2**20),
        cost_estimate=pl.CostEstimate(
            flops=2 * TOK * depth * weight.shape[1], bytes_accessed=2 * depth * weight.shape[1],
            transcendentals=0),
        name="project",
    )(groups, weight, *operands)


def per_device(queries, keys, values, doc_lengths, out_weight):
    zh, y, x, zl, c = (lax.axis_index(a) for a in ("zh", "y", "x", "zl", "c"))
    table = jnp.concatenate([jnp.stack([zh, y, x, c]).astype(jnp.int32), doc_lengths])
    native = join(keys, values)
    other = swap(native, "zh")
    natives = [native] + [move(native, 0, -k) for k in OFFSETS[1:]]
    others = [other] + [move(other, 0, -k) for k in OFFSETS[1:]]
    rings = [ring(native, step) for step in range(1, 1 + NEAR_BLOCKS)]
    own, *sent, is_far = pack(table, natives, others, rings)
    messages = [move(block, -k, 0) for block, k in zip(sent, OFFSETS[1:])]
    nothing = jnp.zeros((FAR_BLOCKS * TOK, 2 * HD), jnp.bfloat16)

    def fetch(block):
        def step(index, carry):
            block, blocks = carry
            block = ring(block, 1)
            at = jnp.maximum(index - NEAR_BLOCKS, 0) * TOK
            return block, lax.dynamic_update_slice_in_dim(blocks, block, at, 0)

        return lax.fori_loop(0, NEAR_BLOCKS + FAR_BLOCKS, step, (block, nothing))[1]

    beyond_rings = lax.cond(is_far[0] == 1, fetch, lambda block: nothing, native)
    rows, *state = attend_own(table, queries, own)
    small = attend_small((table, is_far), (queries, native, *rings, beyond_rings, rows))
    state = attend_middle(table, rows, messages[:2], state, small)
    (first, middle), (second, _) = CHUNKS
    some, rest = attend_last(
        first, middle, table, (rows, own, *messages, small, *state), (queries, *natives))
    chunks = [some] + list(attend_last(
        second, HEADS, table, (rows, own, *messages, rest, *state), ()))
    across = [swap(part, "zl") for part in chunks]
    beside = [swap(part, "c") for part in chunks]
    group = (zl * 2 + c).astype(jnp.int32)
    groups = jnp.stack([group, group ^ 1, group ^ 2, group ^ 3])
    mixed, weight = project(
        [(0, first), (0, second), (1, first), (1, second)], groups, out_weight, chunks + beside)
    across, mixed = lax.optimization_barrier((across, mixed))
    beyond = [swap(part, "c") for part in across]
    return project(
        [(2, first), (3, first), (2, second), (3, second)], groups, weight,
        [across[0], beyond[0], across[1], beyond[1]], mixed)[0]


def solution(mesh):
    fine = Mesh(np.asarray(mesh.devices).reshape(2, 4, 4, 2, 2), ("zh", "y", "x", "zl", "c"))
    seq, kv = ("zh", "y", "x"), ("zl", "c")
    return jax.shard_map(
        per_device,
        mesh=fine,
        in_specs=(P(seq, kv), P(seq, kv), P(seq, kv), P(), P(None, kv)),
        out_specs=P(seq, kv),
        check_vma=False,
    )
```
